256 devices in a mesh: rep: 4 (over x_lo, core), cls: 64 (over x_hi, y, z).
Axes of the slice: x: 4 (x_hi: 2, x_lo: 2; x = x_hi * 2 + x_lo), y: 4, z: 8, core: 2. Of those that a mesh axis runs over, the one named last changes fastest.
Arguments:
- features: bfloat16 [8192, 512], P(('rep', 'cls')), may hold values from -6 to 6
- centers: bfloat16 [131072, 512], P('cls'), may hold values from -0.25 to 0.25
- momentum: float32 [131072, 512], P('cls'), may hold values from -6 to 6
- sample_rows: int32 [98304], P('cls'), may hold values from 0 to 2047, as said below
- labels: int32 [8192], P(('rep', 'cls')), may hold values from 0 to 131071, as said below
Outputs:
- feature_grad: float32 [8192, 512], P(('rep', 'cls'))
- sample_loss: float32 [8192], P(('rep', 'cls'))
- new_centers: bfloat16 [98304, 512], P('cls')
- new_momentum: float32 [98304, 512], P('cls')
The draws below stay inside these ranges and needn't reach their ends.
Inputs may be any that keep to these rules, and one draw needn't show every extreme that they name: `sample_rows`: within each class shard's block of 1536 entries the rows are distinct, and 0 and 2047 are among them. `labels`: each label is k * 2048 + r for a shard k and a row r in shard k's block of sample_rows.
All inputs are finite; a program needn't handle non-finite values.
Results may differ from the reference program's by a relative error of at most 0.011.
Values may be sent and summed in bfloat16 or wider, within the bound.
A program may use at most 128 MiB of HBM per device.

```python
import jax
import jax.numpy as jnp
from jax import lax

D = 512
SAMP_DEV = 1536
CLS_DEV = 2048
TOK_DEV = 32
TOKENS = 8192
CLASSES = 131072
SAMPLED = 98304
N_REP = 4
N_CLS = 64


def shard_picks(key):
    shards_all = SAMPLED // SAMP_DEV
    first_keys = jax.random.split(jax.random.fold_in(key, 1), shards_all)
    second_keys = jax.random.split(jax.random.fold_in(key, 2), shards_all)

    def one_shard(first_key, second_key):
        middle = jax.random.permutation(first_key, CLS_DEV - 2)[:SAMP_DEV - 2].astype(jnp.int32) + 1
        ends = jnp.array([0, CLS_DEV - 1], jnp.int32)
        picked = jnp.concatenate([ends, middle])
        return picked[jax.random.permutation(second_key, SAMP_DEV)]
    return jax.vmap(one_shard)(first_keys, second_keys)


def draw_sample_rows(key, part):
    picked = shard_picks(key)
    return picked.reshape(-1).astype(jnp.int32)


def draw_labels(key, part):
    picked = shard_picks(key)
    key = jax.random.fold_in(key, 11)
    shard_key, slot_key, first_key, second_key = jax.random.split(key, 4)
    shards_all = SAMPLED // SAMP_DEV
    which_shard = jax.random.randint(shard_key, (TOKENS,), 0, shards_all)
    which_slot = jax.random.randint(slot_key, (TOKENS,), 0, SAMP_DEV)
    drawn = (which_shard * CLS_DEV + picked[which_shard, which_slot]).astype(jnp.int32)
    low_place = jax.random.randint(first_key, (), 0, TOKENS)
    high_place = (low_place + 1 + jax.random.randint(second_key, (), 0, TOKENS - 1)) % TOKENS
    drawn = drawn.at[low_place].set(jnp.int32(0))
    drawn = drawn.at[high_place].set(jnp.int32(shards_all * CLS_DEV - 1))
    return drawn.astype(jnp.int32)


def levels(stream_key, dims, pieces, low, top_value):
    loudness = 1.0
    for dim, parts in pieces:
        steps = jax.random.uniform(jax.random.fold_in(jax.random.fold_in(stream_key, 6), dim), (parts,), jnp.float32, low / len(pieces), top_value / len(pieces))
        loudness = loudness * jnp.repeat(jnp.exp(steps), dims[dim] // parts).reshape((-1,) + (1,) * (len(dims) - 1 - dim))
    return loudness


def noise(own_key, extent, spread, limit, cuts=(), held_as=jnp.bfloat16):
    values = spread * jax.random.normal(own_key, extent, jnp.float32)
    if cuts:
        values = values * levels(own_key, extent, cuts, -0.22, 0.18)
    return jnp.clip(values, -limit, limit).astype(held_as)


def setup_inputs(seed: int = 0) -> dict:
    key_of = jax.random.split(jax.random.key(seed), 6)
    return {
        "features": noise(key_of[0], (TOKENS, D), 1.0, 6.0, ((0, 256),)),
        "centers": noise(key_of[1], (CLASSES, D), D ** -0.5, 0.25, ((0, 64),)),
        "momentum": noise(key_of[2], (CLASSES, D), 1.0, 6.0, ((0, 64),), jnp.float32),
        "sample_rows": draw_sample_rows(jax.random.fold_in(key_of[5], 71), 0),
        "labels": draw_labels(jax.random.fold_in(key_of[5], 71), 0),
    }


eps = 1e-06
logit_scale = 64.0
margin = 0.35
moment_rate = 0.9
learn_rate = 0.1

def normalise(values):
    floats = values.astype(jnp.float32)
    norm = jnp.sqrt(lax.optimization_barrier(jnp.sum(floats * floats, axis=-1, keepdims=True)) + eps)
    return (floats / norm, norm)

def apply_update(grad, rows_w, rows_m):
    unit, norm = normalise(rows_w)
    step_dir = (grad - unit * lax.optimization_barrier(jnp.sum(unit * grad, axis=1, keepdims=True))) / norm
    new_m = moment_rate * rows_m + step_dir
    new_w = (rows_w.astype(jnp.float32) - learn_rate * new_m).astype(jnp.bfloat16)
    return (new_w, new_m)

def reference(features, centers, momentum, sample_rows, labels):
    unit_feat, feat_norm = normalise(features)
    feat_bf = unit_feat.astype(jnp.bfloat16)
    picked = sample_rows.reshape(N_CLS, SAMP_DEV)
    global_ids = picked + (jnp.arange(N_CLS, dtype=jnp.int32) * CLS_DEV)[:, None]
    flat_ids = global_ids.reshape(-1)
    center_rows = centers[flat_ids]
    moment_rows = momentum[flat_ids]
    unit_cent, cent_norm = normalise(center_rows)
    cent_bf = unit_cent.astype(jnp.bfloat16).reshape(N_CLS, SAMP_DEV, D)
    group = N_CLS * TOK_DEV
    feats_grp = feat_bf.reshape(N_REP, group, D)
    labels_grp = labels.reshape(N_REP, group)
    grad_cent = jnp.zeros((N_CLS, SAMP_DEV, D), jnp.float32)
    feat_grads = []
    losses = []
    for replica in range(N_REP):
        feats = feats_grp[replica]
        labs = labels_grp[replica]

        def shard_logits(inputs):
            block, class_ids = inputs
            cosine = jnp.dot(feats, block.T, preferred_element_type=jnp.float32)
            matches = (labs[:, None] == class_ids[None, :]).astype(jnp.float32)
            logits = logit_scale * (cosine - margin * matches)
            return (jnp.exp(logits - logit_scale), lax.optimization_barrier(jnp.sum(matches * logits, axis=1)))
        expo, positive = lax.map(shard_logits, (cent_bf, global_ids))
        totals = lax.optimization_barrier(jnp.sum(lax.optimization_barrier(jnp.sum(expo, axis=2)), axis=0))
        positive = lax.optimization_barrier(jnp.sum(positive, axis=0))
        losses.append(jnp.log(totals) + logit_scale - positive)

        def shard_grads(carry, inputs):
            weights_exp, block, class_ids = inputs
            matches = (labs[:, None] == class_ids[None, :]).astype(jnp.float32)
            soft = (weights_exp / totals[:, None] - matches).astype(jnp.bfloat16)
            carry = carry + logit_scale * jnp.dot(soft, block, preferred_element_type=jnp.float32)
            cent_term = logit_scale * lax.dot_general(soft, feats, (((0,), (0,)), ((), ())), preferred_element_type=jnp.float32)
            return (carry, cent_term)
        feat_acc, cent_terms = lax.scan(shard_grads, jnp.zeros((group, D), jnp.float32), (expo, cent_bf, global_ids))
        grad_cent = grad_cent + cent_terms
        feat_grads.append(feat_acc)
    grad_unit = jnp.concatenate(feat_grads, axis=0)
    feature_grad = (grad_unit - unit_feat * lax.optimization_barrier(jnp.sum(unit_feat * grad_unit, axis=1, keepdims=True))) / feat_norm
    new_centers, new_momentum = apply_update(grad_cent.reshape(SAMPLED, D), center_rows, moment_rows)
    return (feature_grad, jnp.concatenate(losses, axis=0), new_centers, new_momentum)
```

```python
import math

import jax
import jax.numpy as jnp
from jax import lax
from jax.experimental import pallas as pl
from jax.experimental.pallas import tpu as pltpu
from jax.sharding import PartitionSpec as P

MESH = pl.DeviceIdType.MESH

EPS = 1e-06
SCALE = 64.0
MARGIN = 0.35
MOMENT_RATE = 0.9
LEARN_RATE = 0.1

NX, NY, NZ = 2, 4, 8
TOK = 32
HALF = TOK // 2
GROUP = TOK * NX * NY * NZ
D = 512
SLOTS = 1536
ROWS = 2048
SB = 256
NSB = SLOTS // SB
OWN = SLOTS // 2
NCB = OWN // SB
LANES = 128
LOG2E = math.log2(math.e)
F32, BF16 = jnp.float32, jnp.bfloat16


class Sems:
    def __init__(self):
        self.n = 0

    def take(self, count):
        first = self.n
        self.n += count
        return first


_s = Sems()
AG1A, AG1B = _s.take(7), _s.take(15)
AGAP, AGAM, AGBP, AGBM = _s.take(4), _s.take(3), _s.take(2), _s.take(1)
LAB1, LAB2, TOT1, TOT2 = _s.take(7), _s.take(7), _s.take(7), _s.take(7)
CORE1, XLO, CORE2 = _s.take(3), _s.take(3), _s.take(3)
RSAP, RSAM, RSBP, RSBM = _s.take(4), _s.take(3), _s.take(2), _s.take(1)
RS2A, RS2B = _s.take(7), _s.take(15)
N_SEMS = _s.n


def wrap(value, n):
    return lax.rem(value + n, n)


def rows16(start, count):
    return pl.ds(pl.multiple_of(start, 16), count)


def lanes(start, count):
    return pl.ds(pl.multiple_of(start, LANES), count)


def row_norm(floats):
    return jnp.sqrt(jnp.sum(floats * floats, axis=-1, keepdims=True) + EPS)


def kernel(
    feat_ref, ids_ref, lab_ref, rows_ref, cent_hbm, mom_hbm,
    fgrad_ref, loss_ref, newc_ref, newm_ref,
    cent_v, mom_v, feats, crow, cbf, cbt, momg, expo, soft, ut,
    labs, lab1, lab1s, lab2, tot, tot1, tot1s, tot2, rtot,
    csend, cown, crecv, xsend, xrecv, gsum,
    sap, rap, sam, ram, sbp, rbp, sbm, rbm,
    wa, wb, wab, wbb, r2a, r2b,
    ssem, rsem, lsem,
):
    rep, cls = lax.axis_index("rep"), lax.axis_index("cls")
    x, y, z = lax.div(cls, NY * NZ), lax.rem(lax.div(cls, NZ), NY), lax.rem(cls, NZ)
    x_lo, core = lax.div(rep, 2), lax.rem(rep, 2)

    def at(x, y, z):
        return (rep, (x * NY + y) * NZ + z)

    xy = [(k % NX, k // NX) for k in range(1, NX * NY)]
    xz = [(k % NX, k // NX) for k in range(1, NX * NZ)]

    def flip(dx):
        return x if dx == 0 else 1 - x

    def xy_to(dx, dy):
        return flip(dx), wrap(y + dy, NY)

    def xy_from(dx, dy):
        return flip(dx), wrap(y - dy, NY)

    def xz_to(dx, dz):
        return flip(dx), wrap(z + dz, NZ)

    def xz_from(dx, dz):
        return flip(dx), wrap(z - dz, NZ)

    core_peer = (x_lo * 2 + 1 - core, cls)
    xlo_peer = ((1 - x_lo) * 2 + core, cls)
    up_z, down_z = at(x, y, wrap(z + 1, NZ)), at(x, y, wrap(z - 1, NZ))
    up_y, down_y = at(x, wrap(y + 1, NY), z), at(x, wrap(y - 1, NY), z)

    pending = []

    def push(src, dst, sem, device):
        copy = pltpu.make_async_remote_copy(
            src_ref=src, dst_ref=dst, send_sem=ssem.at[sem], recv_sem=rsem.at[sem],
            device_id=device, device_id_type=MESH,
        )
        copy.start()
        pending.append(copy)

    def arrived(dst, sem):
        pltpu.make_async_remote_copy(
            src_ref=dst, dst_ref=dst, send_sem=ssem.at[sem], recv_sem=rsem.at[sem],
            device_id=core_peer, device_id_type=MESH,
        ).wait_recv()

    load_c = pltpu.make_async_copy(cent_hbm, cent_v, lsem.at[0])
    load_m = pltpu.make_async_copy(mom_hbm, mom_v, lsem.at[1])
    load_c.start()
    load_m.start()

    barrier = pltpu.get_barrier_semaphore()
    greet = [at(*xy_to(dx, dy), z) for dx, dy in xy]
    greet += [at(xz_to(dx, dz)[0], y, xz_to(dx, dz)[1]) for dx, dz in xz if dz != 0]
    greet += [core_peer, xlo_peer]
    for device in greet:
        pl.semaphore_signal(barrier, inc=1, device_id=device, device_id_type=MESH)

    def row_a(x, y, z):
        return z * 128 + (x * NY + y) * HALF

    def row_b(x, y, z):
        return GROUP // 2 + y * 256 + (x * NZ + z) * HALF

    floats = feat_ref[...].astype(F32)
    unit = (floats / row_norm(floats)).astype(BF16)
    own_a, own_b = rows16(row_a(x, y, z), HALF), rows16(row_b(x, y, z), HALF)
    feats[own_a, :] = unit[:HALF]
    feats[own_b, :] = unit[HALF:]

    pl.semaphore_wait(barrier, len(greet))

    for k, off in enumerate(xy):
        px, py = xy_to(*off)
        push(feats.at[own_a, :], feats.at[own_a, :], AG1A + k, at(px, py, z))
    for k, off in enumerate(xy):
        px, py = xy_to(*off)
        push(lab_ref, lab1.at[k], LAB1 + k, at(px, py, z))
    for k, off in enumerate(xz):
        px, pz = xz_to(*off)
        push(feats.at[own_b, :], feats.at[own_b, :], AG1B + k, at(px, y, pz))

    load_c.wait()

    def pick(sb, carry):
        part = pl.ds(pl.multiple_of(sb * SB, SB), SB)
        ids = ids_ref[part, :] - cls * ROWS
        col = lax.broadcasted_iota(jnp.int32, (SB, LANES), 1)
        hot = jnp.concatenate(
            [jnp.where(ids == col + j * LANES, 1.0, 0.0).astype(BF16) for j in range(ROWS // LANES)],
            axis=1,
        )
        got = jnp.dot(hot, cent_v[...], preferred_element_type=F32)
        crow[part, :] = got.astype(BF16)
        cbf[part, :] = (got / row_norm(got)).astype(BF16)
        return carry

    lax.fori_loop(0, NSB, pick, 0)

    for k, off in enumerate(xy):
        px, py = xy_from(*off)
        arrived(feats.at[rows16(row_a(px, py, z), HALF), :], AG1A + k)

    def blk_a(zb):
        return feats.at[rows16(zb * 128, 128), :]

    def blk_b(yb):
        return feats.at[rows16(GROUP // 2 + yb * 256, 256), :]

    push(blk_a(z), blk_a(z), AGAP, up_z)
    push(blk_a(z), blk_a(z), AGAM, down_z)
    for k, off in enumerate(xz):
        px, pz = xz_from(*off)
        arrived(feats.at[rows16(row_b(px, y, pz), HALF), :], AG1B + k)
    push(blk_b(y), blk_b(y), AGBP, up_y)
    push(blk_b(y), blk_b(y), AGBM, down_y)

    for k in range(7):
        arrived(lab1.at[k], LAB1 + k)
    lab1s[...] = lab_ref[...] + sum(lab1[k] for k in range(7))
    for k in range(7):
        push(lab1s, lab2.at[k], LAB2 + k, at(x, y, wrap(z + k + 1, NZ)))
    for k in range(7):
        arrived(lab2.at[k], LAB2 + k)
    labs[...] = lab1s[...] + sum(lab2[k] for k in range(7))

    def logits(start, nb, lrow):
        n = nb // LANES
        block = feats[rows16(start, nb), :]
        rows = [labs[pl.ds(lrow + h, 1), :] for h in range(n)]

        def body(sb, carry):
            part = pl.ds(pl.multiple_of(sb * SB, SB), SB)
            cosine = lax.dot_general(
                cbf[part, :], block, (((1,), (1,)), ((), ())), preferred_element_type=F32
            )
            ids = ids_ref[part, :]
            out = []
            for h in range(n):
                cos_h = cosine[:, h * LANES : (h + 1) * LANES]
                match = ids == rows[h]
                logit = SCALE * (cos_h - jnp.where(match, MARGIN, 0.0))
                e = jnp.exp2((logit - SCALE) * LOG2E)
                expo[part, lanes(start + h * LANES, LANES)] = e
                out.append(carry[2 * h] + jnp.sum(e.reshape(SB // 8, 8, LANES), axis=0))
                hit = jnp.where(match, logit, 0.0)
                out.append(carry[2 * h + 1] + jnp.sum(hit.reshape(SB // 8, 8, LANES), axis=0))
            return tuple(out)

        zero = jnp.zeros((8, LANES), F32)
        sums = lax.fori_loop(0, NSB, body, (zero,) * (2 * n))
        for h in range(n):
            tot[pl.ds(lrow + h, 1), :] = jnp.sum(sums[2 * h], axis=0, keepdims=True)
            tot[pl.ds(16 + lrow + h, 1), :] = jnp.sum(sums[2 * h + 1], axis=0, keepdims=True)

    def logits_a(zb):
        logits(zb * 128, 128, zb)

    def logits_b(yb):
        logits(GROUP // 2 + yb * 256, 256, 8 + yb * 2)

    logits_a(z)
    logits_b(y)
    for s in range(4):
        zp, zm = wrap(z - 1 - s, NZ), wrap(z + 1 + s, NZ)
        arrived(blk_a(zp), AGAP + s)
        if s < 3:
            push(blk_a(zp), blk_a(zp), AGAP + s + 1, up_z)
            arrived(blk_a(zm), AGAM + s)
        if s < 2:
            push(blk_a(zm), blk_a(zm), AGAM + s + 1, down_z)
        if s == 1:
            yp, ym = wrap(y - 1, NY), wrap(y + 1, NY)
            arrived(blk_b(yp), AGBP)
            push(blk_b(yp), blk_b(yp), AGBP + 1, up_y)
        logits_a(zp)
        if s < 3:
            logits_a(zm)
        if s == 1:
            arrived(blk_b(ym), AGBM)
            logits_b(yp)
            logits_b(ym)
    y2 = wrap(y - 2, NY)
    arrived(blk_b(y2), AGBP + 1)
    logits_b(y2)

    for k, off in enumerate(xy):
        px, py = xy_to(*off)
        push(tot, tot1.at[k], TOT1 + k, at(px, py, z))

    load_m.wait()

    def pick_m(j, carry):
        for u in range(16):
            i = j * 16 + u
            momg[pl.ds(i, 1), :] = mom_v[pl.ds(rows_ref[i], 1), :]
        return carry

    lax.fori_loop(0, SLOTS // 32, pick_m, 0)
    for k in range(7):
        arrived(tot1.at[k], TOT1 + k)
    tot1s[...] = tot[...] + sum(tot1[k] for k in range(7))
    for k in range(7):
        push(tot1s, tot2.at[k], TOT2 + k, at(x, y, wrap(z + k + 1, NZ)))

    lax.fori_loop(SLOTS // 32, SLOTS // 16, pick_m, 0)
    for sb in range(NSB):
        cbt[:, sb * SB : (sb + 1) * SB] = cbf[sb * SB : (sb + 1) * SB, :].T

    for k in range(7):
        arrived(tot2.at[k], TOT2 + k)
    whole = tot1s[...] + sum(tot2[k] for k in range(7))
    totals, positive = whole[:16], whole[16:]
    rtot[...] = 1.0 / totals
    loss_ref[...] = jnp.log(totals) + SCALE - positive

    def center_grad(first):
        part = pl.ds(pl.multiple_of(first, SB), SB)
        ids = ids_ref[part, :]

        def body(k, carry):
            col = lanes(k * LANES, LANES)
            match = ids == labs[pl.ds(k, 1), :]
            value = expo[part, col] * rtot[pl.ds(k, 1), :]
            soft[part, col] = (value - jnp.where(match, 1.0, 0.0)).astype(BF16)
            return carry

        lax.fori_loop(0, GROUP // LANES, body, 0)
        return SCALE * jnp.dot(soft[part, :], feats[...], preferred_element_type=F32)

    mine, other = core * OWN, (1 - core) * OWN

    def join_cores(i):
        arrived(crecv.at[i], CORE1 + i)
        xsend[i] = (cown[i].astype(F32) + crecv[i].astype(F32)).astype(BF16)
        push(xsend.at[i], xrecv.at[i], XLO + i, xlo_peer)

    for i in range(NCB):
        csend[i] = center_grad(other + i * SB).astype(BF16)
        push(csend.at[i], crecv.at[i], CORE1 + i, core_peer)
        cown[i] = center_grad(mine + i * SB).astype(BF16)
        if i:
            join_cores(i - 1)
    join_cores(NCB - 1)

    def feature_part(k, carry):
        col = lanes(k * 256, 256)
        ut[:, col] = SCALE * jnp.dot(cbt[...], soft[:, col], preferred_element_type=F32)
        return carry

    lax.fori_loop(0, GROUP // 256, feature_part, 0)

    def part_a(zb):
        return ut[:, lanes(wrap(zb, NZ) * 128, 128)]

    def part_b(yb):
        return ut[:, lanes(GROUP // 2 + wrap(yb, NY) * 256, 256)]

    def step_a(s):
        plus = part_a(z + 4 - s)
        if s:
            arrived(rap.at[s - 1], RSAP + s - 1)
            plus = plus + rap[s - 1].astype(F32)
        sap[s] = plus.astype(BF16)
        push(sap.at[s], rap.at[s], RSAP + s, up_z)
        if s < 3:
            minus = part_a(z - 3 + s)
            if s:
                arrived(ram.at[s - 1], RSAM + s - 1)
                minus = minus + ram[s - 1].astype(F32)
            sam[s] = minus.astype(BF16)
            push(sam.at[s], ram.at[s], RSAM + s, down_z)

    def step_b(s):
        plus = part_b(y + 2 - s)
        if s:
            arrived(rbp.at[s - 1], RSBP + s - 1)
            plus = plus + rbp[s - 1].astype(F32)
        sbp[s] = plus.astype(BF16)
        push(sbp.at[s], rbp.at[s], RSBP + s, up_y)
        if s == 0:
            sbm[0] = part_b(y - 1).astype(BF16)
            push(sbm.at[0], rbm.at[0], RSBM, down_y)

    step_a(0)
    step_b(0)
    step_a(1)
    step_a(2)
    step_b(1)
    step_a(3)
    arrived(ram.at[2], RSAM + 2)
    arrived(rap.at[3], RSAP + 3)
    slab = part_a(z) + rap[3].astype(F32) + ram[2].astype(F32)
    wa[...] = slab.T
    wab[...] = wa[...].astype(BF16)
    for k, off in enumerate(xy):
        px, py = xy_to(*off)
        piece = rows16((px * NY + py) * HALF, HALF)
        push(wab.at[piece, :], r2a.at[k], RS2A + k, at(px, py, z))
    arrived(rbm.at[0], RSBM)
    arrived(rbp.at[1], RSBP + 1)
    slab = part_b(y) + rbp[1].astype(F32) + rbm[0].astype(F32)
    wb[...] = slab.T
    wbb[...] = wb[...].astype(BF16)
    for k, off in enumerate(xz):
        px, pz = xz_to(*off)
        piece = rows16((px * NZ + pz) * HALF, HALF)
        push(wbb.at[piece, :], r2b.at[k], RS2B + k, at(px, y, pz))

    for i in range(NCB):
        arrived(xrecv.at[i], XLO + i)
        both = xsend[i].astype(F32) + xrecv[i].astype(F32)
        place = gsum.at[rows16(mine + i * SB, SB), :]
        gsum[rows16(mine + i * SB, SB), :] = both.astype(BF16)
        push(place, place, CORE2 + i, core_peer)

    def update(first):
        part = pl.ds(pl.multiple_of(first, SB), SB)
        rows = crow[part, :].astype(F32)
        norm = row_norm(rows)
        unit_c = rows / norm
        grad = gsum[part, :].astype(F32)
        step = (grad - unit_c * jnp.sum(unit_c * grad, axis=1, keepdims=True)) / norm
        new_m = MOMENT_RATE * momg[part, :] + step
        newm_ref[part, :] = new_m
        newc_ref[part, :] = (rows - LEARN_RATE * new_m).astype(BF16)

    for i in range(NCB):
        update(mine + i * SB)

    for k in range(7):
        arrived(r2a.at[k], RS2A + k)
    g_a = wa[pl.ds(pl.multiple_of((x * NY + y) * HALF, HALF), HALF), :]
    g_a = g_a + sum(r2a[k].astype(F32) for k in range(7))
    for k in range(15):
        arrived(r2b.at[k], RS2B + k)
    g_b = wb[pl.ds(pl.multiple_of((x * NZ + z) * HALF, HALF), HALF), :]
    g_b = g_b + sum(r2b[k].astype(F32) for k in range(15))
    for h, grad in enumerate((g_a, g_b)):
        own = feat_ref[h * HALF : (h + 1) * HALF, :].astype(F32)
        norm = row_norm(own)
        unit_f = own / norm
        dot = jnp.sum(unit_f * grad, axis=1, keepdims=True)
        fgrad_ref[h * HALF : (h + 1) * HALF, :] = (grad - unit_f * dot) / norm

    for i in range(NCB):
        arrived(gsum.at[rows16(other + i * SB, SB), :], CORE2 + i)
        update(other + i * SB)

    for copy in pending:
        copy.wait_send()


def local(features, centers, momentum, sample_rows, labels):
    cls = lax.axis_index("cls")
    x, y, z = cls // (NY * NZ), cls // NZ % NY, cls % NZ
    ids = jnp.broadcast_to((sample_rows + cls * ROWS)[:, None], (SLOTS, LANES))
    place = jnp.arange(GROUP // HALF, dtype=jnp.int32)
    at_a = z * 8 + x * NY + y
    at_b = GROUP // TOK + y * 16 + x * NZ + z
    placed = jnp.where(
        (place == at_a)[:, None],
        labels[None, :HALF],
        jnp.where((place == at_b)[:, None], labels[None, HALF:], 0),
    ).reshape(16, LANES)

    vm = pl.BlockSpec(memory_space=pltpu.VMEM)
    hbm = pl.BlockSpec(memory_space=pl.ANY)
    v = pltpu.VMEM
    f_grad, loss, new_c, new_m = pl.pallas_call(
        kernel,
        out_shape=(
            jax.ShapeDtypeStruct((TOK, D), F32),
            jax.ShapeDtypeStruct((16, LANES), F32),
            jax.ShapeDtypeStruct((SLOTS, D), BF16),
            jax.ShapeDtypeStruct((SLOTS, D), F32),
        ),
        in_specs=[vm, vm, vm, pl.BlockSpec(memory_space=pltpu.SMEM), hbm, hbm],
        out_specs=(vm, vm, vm, vm),
        scratch_shapes=[
            v((ROWS, D), BF16), v((ROWS, D), F32), v((GROUP, D), BF16),
            v((SLOTS, D), BF16), v((SLOTS, D), BF16), v((D, SLOTS), BF16), v((SLOTS, D), F32),
            v((SLOTS, GROUP), F32), v((SLOTS, GROUP), BF16), v((D, GROUP), F32),
            v((16, LANES), jnp.int32), v((7, 16, LANES), jnp.int32), v((16, LANES), jnp.int32),
            v((7, 16, LANES), jnp.int32),
            v((32, LANES), F32), v((7, 32, LANES), F32), v((32, LANES), F32), v((7, 32, LANES), F32),
            v((16, LANES), F32),
            v((NCB, SB, D), BF16), v((NCB, SB, D), BF16), v((NCB, SB, D), BF16),
            v((NCB, SB, D), BF16), v((NCB, SB, D), BF16), v((SLOTS, D), BF16),
            v((4, D, 128), BF16), v((4, D, 128), BF16), v((3, D, 128), BF16), v((3, D, 128), BF16),
            v((2, D, 256), BF16), v((2, D, 256), BF16), v((1, D, 256), BF16), v((1, D, 256), BF16),
            v((128, D), F32), v((256, D), F32), v((128, D), BF16), v((256, D), BF16),
            v((7, HALF, D), BF16), v((15, HALF, D), BF16),
            pltpu.SemaphoreType.DMA((N_SEMS,)), pltpu.SemaphoreType.DMA((N_SEMS,)),
            pltpu.SemaphoreType.DMA((2,)),
        ],
        compiler_params=pltpu.CompilerParams(
            collective_id=0, has_side_effects=True, vmem_limit_bytes=60 * 1024 * 1024
        ),
    )(features, ids, placed, sample_rows, centers, momentum)
    flat = loss.reshape(GROUP // HALF, HALF)
    own = jnp.concatenate(
        [
            lax.dynamic_slice_in_dim(flat, at_a, 1),
            lax.dynamic_slice_in_dim(flat, at_b, 1),
        ],
        axis=0,
    ).reshape(TOK)
    return (f_grad, own, new_c, new_m)


def solution(mesh):
    in_specs = (
        P(("rep", "cls"), None),
        P("cls", None),
        P("cls", None),
        P("cls"),
        P(("rep", "cls")),
    )
    out_specs = (P(("rep", "cls"), None), P(("rep", "cls")), P("cls", None), P("cls", None))
    return jax.shard_map(local, mesh=mesh, in_specs=in_specs, out_specs=out_specs, check_vma=False)
```

```python
import math

import jax
import jax.numpy as jnp
from jax import lax
from jax.experimental import pallas as pl
from jax.experimental.pallas import tpu as pltpu
from jax.sharding import PartitionSpec as P

MESH = pl.DeviceIdType.MESH

EPS = 1e-06
SCALE = 64.0
MARGIN = 0.35
MOMENT_RATE = 0.9
LEARN_RATE = 0.1

NX, NY, NZ = 2, 4, 8
TOK = 32
HALF = TOK // 2
GROUP = TOK * NX * NY * NZ
D = 512
SLOTS = 1536
ROWS = 2048
SB = 256
NSB = SLOTS // SB
OWN = SLOTS // 2
NCB = OWN // SB
LANES = 128
LOG2E = math.log2(math.e)
F32, BF16 = jnp.float32, jnp.bfloat16


class Sems:
    def __init__(self):
        self.n = 0

    def take(self, count):
        first = self.n
        self.n += count
        return first


_s = Sems()
AG1A, AG1B, AG2B = _s.take(7), _s.take(7), _s.take(7)
AGAP, AGAM = _s.take(4), _s.take(3)
LAB1, LAB2, TOT1, TOT2, POS1, POS2 = (_s.take(7) for _ in range(6))
CORE1, XLO, CORE2 = _s.take(3), _s.take(3), _s.take(3)
RSAP, RSAM, RSB = _s.take(4), _s.take(3), _s.take(3)
RS2A, RSBX, RSBZ = _s.take(7), _s.take(1), _s.take(7)
N_SEMS = _s.n


def wrap(value, n):
    return lax.rem(value + n, n)


def rows16(start, count):
    return pl.ds(pl.multiple_of(start, 16), count)


def lanes(start, count):
    return pl.ds(pl.multiple_of(start, LANES), count)


def row_norm(floats):
    return jnp.sqrt(jnp.sum(floats * floats, axis=-1, keepdims=True) + EPS)


def kernel(
    feat_ref, rowv_ref, lab_ref, rows_ref, cent_hbm, mom_hbm,
    fgrad_ref, loss_ref, crow_hbm, momg_hbm, gsum_hbm,
    cent_v, mom_v, feats, ids_ref, crow, cbf, cbt, momg, expo, soft,
    place, labs, lab1, lab1s, lab2, tot, tot1, tot1s, tot2, rtot, pos1, pos1s, pos2,
    csend, cown, crecv, xsend, xrecv, gown,
    ua, ub, sap, rap, sam, ram, sb_, rb_,
    wa, wb, wab, wbb, wbz, wbzb, r2a, rbx, rbz,
    ssem, rsem, lsem,
):
    rep, cls = lax.axis_index("rep"), lax.axis_index("cls")
    x, y, z = lax.div(cls, NY * NZ), lax.rem(lax.div(cls, NZ), NY), lax.rem(cls, NZ)
    x_lo, core = lax.div(rep, 2), lax.rem(rep, 2)

    def at(x, y, z):
        return (rep, (x * NY + y) * NZ + z)

    xy = [(k % NX, k // NX) for k in range(1, NX * NY)]

    def flip(dx):
        return x if dx == 0 else 1 - x

    def xy_to(k):
        dx, dy = xy[k]
        return flip(dx), wrap(y + dy, NY)

    def xy_from(k):
        dx, dy = xy[k]
        return flip(dx), wrap(y - dy, NY)

    def z_to(k):
        return wrap(z + k + 1, NZ)

    def z_from(k):
        return wrap(z - k - 1, NZ)

    xy_peers = [at(*xy_to(k), z) for k in range(7)]
    z_peers = [at(x, y, z_to(k)) for k in range(7)]
    y_peers = [at(x, wrap(y + k + 1, NY), z) for k in range(3)]
    x_peer = at(1 - x, y, z)
    core_peer = (x_lo * 2 + 1 - core, cls)
    xlo_peer = ((1 - x_lo) * 2 + core, cls)
    up_z, down_z = z_peers[0], z_peers[6]

    pending = []

    def push(src, dst, sem, device):
        copy = pltpu.make_async_remote_copy(
            src_ref=src, dst_ref=dst, send_sem=ssem.at[sem], recv_sem=rsem.at[sem],
            device_id=device, device_id_type=MESH,
        )
        copy.start()
        pending.append(copy)

    def arrived(dst, sem):
        pltpu.make_async_remote_copy(
            src_ref=dst, dst_ref=dst, send_sem=ssem.at[sem], recv_sem=rsem.at[sem],
            device_id=core_peer, device_id_type=MESH,
        ).wait_recv()

    stores = []

    def store(src, dst, sem):
        copy = pltpu.make_async_copy(src, dst, lsem.at[sem])
        copy.start()
        stores.append(copy)

    barrier = pltpu.get_barrier_semaphore()
    greet = xy_peers + z_peers + [core_peer, xlo_peer]
    for device in greet:
        pl.semaphore_signal(barrier, inc=1, device_id=device, device_id_type=MESH)

    load_c = pltpu.make_async_copy(cent_hbm, cent_v, lsem.at[0])
    load_m = pltpu.make_async_copy(mom_hbm, mom_v, lsem.at[1])
    load_c.start()
    load_m.start()

    half = GROUP // 2
    my_q, my_b = x * NY + y, y * NX + x

    floats = feat_ref[...].astype(F32)
    unit = (floats / row_norm(floats)).astype(BF16)
    own_a = rows16(z * 128 + my_q * HALF, HALF)
    own_b = rows16(half + my_b * 128 + z * HALF, HALF)
    feats[own_a, :] = unit[:HALF]
    feats[own_b, :] = unit[HALF:]

    lane = lax.broadcasted_iota(jnp.int32, (8, LANES), 1)
    row = lax.broadcasted_iota(jnp.int32, (8, LANES), 0)
    lab_a = jnp.broadcast_to(lab_ref[0:1, :], (8, LANES))
    lab_b = jnp.broadcast_to(lab_ref[1:2, :], (8, LANES))
    place[0:8, :] = jnp.where((row == z) & (lane // HALF == my_q), lab_a, 0)
    place[8:16, :] = jnp.where((row == my_b) & (lane // HALF == z), lab_b, 0)

    pl.semaphore_wait(barrier, len(greet))

    for k in range(7):
        push(feats.at[own_a, :], feats.at[own_a, :], AG1A + k, xy_peers[k])
    for k in range(7):
        push(feats.at[own_b, :], feats.at[own_b, :], AG1B + k, z_peers[k])
    for k in range(7):
        push(place, lab1.at[k], LAB1 + k, xy_peers[k])

    for b in range(SLOTS // LANES):
        wide = jnp.broadcast_to(rowv_ref[b : b + 1, :].astype(F32), (LANES, LANES))
        ids_ref[b * LANES : (b + 1) * LANES, :] = wide.T.astype(jnp.int32) + cls * ROWS

    load_c.wait()

    def pick(sb):
        part = slice(sb * SB, (sb + 1) * SB)
        ids = ids_ref[part, :] - cls * ROWS
        col = lax.broadcasted_iota(jnp.int32, (SB, LANES), 1)
        hot = jnp.concatenate(
            [jnp.where(ids == col + j * LANES, 1.0, 0.0).astype(BF16) for j in range(ROWS // LANES)],
            axis=1,
        )
        got = jnp.dot(hot, cent_v[...], preferred_element_type=F32)
        crow[part, :] = got.astype(BF16)
        cbf[part, :] = (got / row_norm(got)).astype(BF16)

    for sb in range(NSB // 2):
        pick(sb)

    def blk_a(zb):
        return feats.at[rows16(zb * 128, 128), :]

    def blk_b(px, py):
        return feats.at[rows16(half + (py * NX + px) * 128, 128), :]

    for k in range(7):
        px, py = xy_from(k)
        arrived(feats.at[rows16(z * 128 + (px * NY + py) * HALF, HALF), :], AG1A + k)
    push(blk_a(z), blk_a(z), AGAP, up_z)
    push(blk_a(z), blk_a(z), AGAM, down_z)
    for k in range(7):
        arrived(feats.at[rows16(half + my_b * 128 + z_from(k) * HALF, HALF), :], AG1B + k)
    for k in range(7):
        push(blk_b(x, y), blk_b(x, y), AG2B + k, xy_peers[k])

    for k in range(7):
        arrived(lab1.at[k], LAB1 + k)
    lab1s[...] = place[...] + sum(lab1[k] for k in range(7))
    for k in range(7):
        push(lab1s, lab2.at[k], LAB2 + k, z_peers[k])

    for sb in range(NSB // 2, NSB):
        pick(sb)
    store(crow, crow_hbm, 2)

    for k in range(7):
        arrived(lab2.at[k], LAB2 + k)
    labs[...] = lab1s[...] + sum(lab2[k] for k in range(7))

    def logits(tiles):
        block = jnp.concatenate([feats[rows16(t * LANES, LANES), :] for t in tiles], axis=0)
        rows = [labs[pl.ds(t, 1), :] for t in tiles]
        sums = [jnp.zeros((8, LANES), F32) for _ in range(4)]
        for sb in range(NSB):
            part = slice(sb * SB, (sb + 1) * SB)
            cosine = lax.dot_general(
                cbf[part, :], block, (((1,), (1,)), ((), ())), preferred_element_type=F32
            )
            ids = ids_ref[part, :]
            for h, t in enumerate(tiles):
                cos_h = cosine[:, h * LANES : (h + 1) * LANES]
                match = ids == rows[h]
                logit = SCALE * (cos_h - jnp.where(match, MARGIN, 0.0))
                e = jnp.exp2((logit - SCALE) * LOG2E)
                expo[part, lanes(t * LANES, LANES)] = e
                sums[h] += jnp.sum(e.reshape(SB // 8, 8, LANES), axis=0)
                hit = jnp.where(match, logit, 0.0)
                sums[2 + h] += jnp.sum(hit.reshape(SB // 8, 8, LANES), axis=0)
        for h, t in enumerate(tiles):
            tot[pl.ds(t, 1), :] = jnp.sum(sums[h], axis=0, keepdims=True)
            tot[pl.ds(16 + t, 1), :] = jnp.sum(sums[2 + h], axis=0, keepdims=True)

    def ring(s):
        zp, zm = wrap(z - 1 - s, NZ), wrap(z + 1 + s, NZ)
        arrived(blk_a(zp), AGAP + s)
        if s < 3:
            push(blk_a(zp), blk_a(zp), AGAP + s + 1, up_z)
            arrived(blk_a(zm), AGAM + s)
        if s < 2:
            push(blk_a(zm), blk_a(zm), AGAM + s + 1, down_z)
        return zp, zm

    def plane(k):
        px, py = xy_from(k)
        arrived(blk_b(px, py), AG2B + k)
        return 8 + py * NX + px

    logits((z, 8 + my_b))
    logits(ring(0))
    logits(ring(1))
    logits((plane(0), plane(1)))
    logits((plane(2), plane(3)))
    logits(ring(2))
    logits((plane(4), plane(5)))
    logits((ring(3)[0], plane(6)))

    t_all, p_all = tot.at[0:16, :], tot.at[16:32, :]
    for k in range(7):
        push(t_all, tot1.at[k], TOT1 + k, xy_peers[k])
    for k in range(7):
        push(p_all, pos1.at[k], POS1 + k, xy_peers[k])

    load_m.wait()

    def pick_m(j, carry):
        for u in range(16):
            i = j * 16 + u
            momg[pl.ds(i, 1), :] = mom_v[pl.ds(rows_ref[i], 1), :]
        return carry

    lax.fori_loop(0, SLOTS // 32, pick_m, 0)
    for k in range(7):
        arrived(tot1.at[k], TOT1 + k)
    tot1s[...] = tot[0:16, :] + sum(tot1[k] for k in range(7))
    for k in range(7):
        push(tot1s, tot2.at[k], TOT2 + k, z_peers[k])
    for k in range(7):
        arrived(pos1.at[k], POS1 + k)
    pos1s[...] = tot[16:32, :] + sum(pos1[k] for k in range(7))
    for k in range(7):
        push(pos1s, pos2.at[k], POS2 + k, z_peers[k])

    lax.fori_loop(SLOTS // 32, SLOTS // 16, pick_m, 0)
    store(momg, momg_hbm, 3)
    for sb in range(NSB):
        cbt[:, sb * SB : (sb + 1) * SB] = cbf[sb * SB : (sb + 1) * SB, :].T

    for k in range(7):
        arrived(tot2.at[k], TOT2 + k)
    totals = tot1s[...] + sum(tot2[k] for k in range(7))
    rtot[...] = 1.0 / totals

    def soften(tiles):
        for t in tiles:
            col = lanes(t * LANES, LANES)
            inverse, lab = rtot[pl.ds(t, 1), :], labs[pl.ds(t, 1), :]
            for sb in range(NSB):
                part = slice(sb * SB, (sb + 1) * SB)
                value = expo[part, col] * inverse
                match = jnp.where(ids_ref[part, :] == lab, 1.0, 0.0)
                soft[part, col] = (value - match).astype(BF16)

    def feature_part(tiles):
        cols = jnp.concatenate([soft[:, lanes(t * LANES, LANES)] for t in tiles], axis=1)
        return SCALE * jnp.dot(cbt[...], cols, preferred_element_type=F32)

    def center_grad(first):
        part = pl.ds(pl.multiple_of(first, SB), SB)
        return (SCALE * jnp.dot(soft[part, :], feats[...], preferred_element_type=F32)).astype(BF16)

    mine, other = core * OWN, (1 - core) * OWN

    def grad_other(i):
        csend[i] = center_grad(other + i * SB)
        push(csend.at[i], crecv.at[i], CORE1 + i, core_peer)

    def grad_mine(i):
        cown[i] = center_grad(mine + i * SB)

    def join_cores(i):
        arrived(crecv.at[i], CORE1 + i)
        xsend[i] = (cown[i].astype(F32) + crecv[i].astype(F32)).astype(BF16)
        push(xsend.at[i], xrecv.at[i], XLO + i, xlo_peer)

    def tiles_a(s):
        return wrap(z + 4 - s, NZ), wrap(z - 3 + s, NZ)

    def tiles_b(yb):
        return 8 + yb * NX, 8 + yb * NX + 1

    def ring_sum(s):
        plus = ua[s][:, :128]
        if s:
            arrived(rap.at[s - 1], RSAP + s - 1)
            plus = plus + rap[s - 1].astype(F32)
        sap[s] = plus.astype(BF16)
        push(sap.at[s], rap.at[s], RSAP + s, up_z)
        if s < 3:
            minus = ua[s][:, 128:]
            if s:
                arrived(ram.at[s - 1], RSAM + s - 1)
                minus = minus + ram[s - 1].astype(F32)
            sam[s] = minus.astype(BF16)
            push(sam.at[s], ram.at[s], RSAM + s, down_z)

    def part_a(s):
        ua[s] = feature_part(tiles_a(s))

    soften(tiles_a(0))
    part_a(0)
    ring_sum(0)
    y_to = [wrap(y + k + 1, NY) for k in range(3)]
    for k in (1, 0, 2):
        soften(tiles_b(y_to[k]))
        sb_[k] = feature_part(tiles_b(y_to[k])).astype(BF16)
        push(sb_.at[k], rb_.at[k], RSB + k, y_peers[k])
    soften(tiles_a(1))
    soften(tiles_a(2))
    soften(tiles_a(3))
    soften(tiles_b(y))
    grad_other(0)
    grad_mine(0)
    part_a(1)
    ring_sum(1)
    grad_other(1)
    join_cores(0)
    grad_mine(1)
    grad_other(2)
    join_cores(1)
    grad_mine(2)
    part_a(2)
    ring_sum(2)
    join_cores(2)
    part_a(3)
    ub[...] = feature_part(tiles_b(y))

    for k in range(7):
        arrived(pos2.at[k], POS2 + k)
    positive = pos1s[...] + sum(pos2[k] for k in range(7))
    loss_ref[...] = jnp.log(totals) + SCALE - positive

    ring_sum(3)

    for k in range(3):
        arrived(rb_.at[k], RSB + k)
    slab = ub[...] + sum(rb_[k].astype(F32) for k in range(3))
    wb[...] = slab.T
    wbb[...] = wb[rows16((1 - x) * 128, 128), :].astype(BF16)
    push(wbb, rbx, RSBX, x_peer)

    arrived(ram.at[2], RSAM + 2)
    arrived(rap.at[3], RSAP + 3)
    slab = ua[3][:, 128:] + rap[3].astype(F32) + ram[2].astype(F32)
    wa[...] = slab.T
    wab[...] = wa[...].astype(BF16)
    for k in range(7):
        px, py = xy_to(k)
        push(wab.at[rows16((px * NY + py) * HALF, HALF), :], r2a.at[k], RS2A + k, xy_peers[k])

    arrived(rbx, RSBX)
    wbz[...] = wb[rows16(x * 128, 128), :] + rbx[...].astype(F32)
    wbzb[...] = wbz[...].astype(BF16)
    for k in range(7):
        push(wbzb.at[rows16(z_to(k) * HALF, HALF), :], rbz.at[k], RSBZ + k, z_peers[k])

    for i in range(NCB):
        arrived(xrecv.at[i], XLO + i)
        gown[i] = (xsend[i].astype(F32) + xrecv[i].astype(F32)).astype(BF16)
        place_i = gsum_hbm.at[rows16(mine + i * SB, SB), :]
        push(gown.at[i], place_i, CORE2 + i, core_peer)
        store(gown.at[i], place_i, 4 + i)

    for k in range(7):
        arrived(r2a.at[k], RS2A + k)
    g_a = wa[rows16(my_q * HALF, HALF), :] + sum(r2a[k].astype(F32) for k in range(7))
    for k in range(7):
        arrived(rbz.at[k], RSBZ + k)
    g_b = wbz[rows16(z * HALF, HALF), :] + sum(rbz[k].astype(F32) for k in range(7))
    for h, grad in enumerate((g_a, g_b)):
        own = feat_ref[h * HALF : (h + 1) * HALF, :].astype(F32)
        norm = row_norm(own)
        unit_f = own / norm
        dot = jnp.sum(unit_f * grad, axis=1, keepdims=True)
        fgrad_ref[h * HALF : (h + 1) * HALF, :] = (grad - unit_f * dot) / norm

    for i in range(NCB):
        arrived(gsum_hbm.at[rows16(other + i * SB, SB), :], CORE2 + i)
    for copy in pending:
        copy.wait_send()
    for copy in stores:
        copy.wait()


def update(crow_ref, momg_ref, gsum_ref, fgrad_ref, loss_ref, newc_ref, newm_ref, fout_ref, lout_ref):
    rows = crow_ref[...].astype(F32)
    norm = row_norm(rows)
    unit = rows / norm
    grad = gsum_ref[...].astype(F32)
    step = (grad - unit * jnp.sum(unit * grad, axis=1, keepdims=True)) / norm
    new_m = MOMENT_RATE * momg_ref[...] + step
    newm_ref[...] = new_m
    newc_ref[...] = (rows - LEARN_RATE * new_m).astype(BF16)
    fout_ref[...] = fgrad_ref[...]
    lout_ref[...] = loss_ref[...]


def local(features, centers, momentum, sample_rows, labels):
    vm = pl.BlockSpec(memory_space=pltpu.VMEM)
    hbm = pl.BlockSpec(memory_space=pl.ANY)
    v = pltpu.VMEM
    sds = jax.ShapeDtypeStruct
    f_grad, loss, crow, momg, gsum = pl.pallas_call(
        kernel,
        out_shape=(
            sds((TOK, D), F32),
            sds((16, LANES), F32),
            sds((SLOTS, D), BF16),
            sds((SLOTS, D), F32),
            sds((SLOTS, D), BF16),
        ),
        in_specs=[vm, vm, vm, pl.BlockSpec(memory_space=pltpu.SMEM), hbm, hbm],
        out_specs=(vm, vm, hbm, hbm, hbm),
        scratch_shapes=[
            v((ROWS, D), BF16), v((ROWS, D), F32), v((GROUP, D), BF16), v((SLOTS, LANES), jnp.int32),
            v((SLOTS, D), BF16), v((SLOTS, D), BF16), v((D, SLOTS), BF16), v((SLOTS, D), F32),
            v((SLOTS, GROUP), F32), v((SLOTS, GROUP), BF16),
            v((16, LANES), jnp.int32), v((16, LANES), jnp.int32), v((7, 16, LANES), jnp.int32),
            v((16, LANES), jnp.int32), v((7, 16, LANES), jnp.int32),
            v((32, LANES), F32), v((7, 16, LANES), F32), v((16, LANES), F32), v((7, 16, LANES), F32),
            v((16, LANES), F32), v((7, 16, LANES), F32), v((16, LANES), F32), v((7, 16, LANES), F32),
            v((NCB, SB, D), BF16), v((NCB, SB, D), BF16), v((NCB, SB, D), BF16),
            v((NCB, SB, D), BF16), v((NCB, SB, D), BF16), v((NCB, SB, D), BF16),
            v((4, D, 256), F32), v((D, 256), F32),
            v((4, D, 128), BF16), v((4, D, 128), BF16), v((3, D, 128), BF16), v((3, D, 128), BF16),
            v((3, D, 256), BF16), v((3, D, 256), BF16),
            v((128, D), F32), v((256, D), F32), v((128, D), BF16), v((128, D), BF16),
            v((128, D), F32), v((128, D), BF16),
            v((7, HALF, D), BF16), v((128, D), BF16), v((7, HALF, D), BF16),
            pltpu.SemaphoreType.DMA((N_SEMS,)), pltpu.SemaphoreType.DMA((N_SEMS,)),
            pltpu.SemaphoreType.DMA((4 + NCB,)),
        ],
        compiler_params=pltpu.CompilerParams(
            collective_id=0, has_side_effects=True, vmem_limit_bytes=60 * 1024 * 1024
        ),
    )(
        features,
        sample_rows.reshape(SLOTS // LANES, LANES),
        jnp.tile(labels.reshape(2, HALF), (1, LANES // HALF)),
        sample_rows,
        centers,
        momentum,
    )
    def rows_of(i):
        return (i, 0)

    def whole(i):
        return (0, 0)

    block = pl.BlockSpec((SB, D), rows_of)
    new_c, new_m, f_grad, loss = pl.pallas_call(
        update,
        grid=(NSB,),
        out_shape=(
            sds((SLOTS, D), BF16), sds((SLOTS, D), F32), sds((TOK, D), F32), sds((16, LANES), F32),
        ),
        in_specs=[block, block, block, pl.BlockSpec((TOK, D), whole), pl.BlockSpec((16, LANES), whole)],
        out_specs=(block, block, pl.BlockSpec((TOK, D), whole), pl.BlockSpec((16, LANES), whole)),
    )(crow, momg, gsum, f_grad, loss)
    cls = lax.axis_index("cls")
    x, y, z = cls // (NY * NZ), cls // NZ % NY, cls % NZ
    flat = loss.reshape(GROUP // HALF, HALF)
    own = jnp.concatenate(
        [
            lax.dynamic_slice_in_dim(flat, z * 8 + x * NY + y, 1),
            lax.dynamic_slice_in_dim(flat, GROUP // TOK + (y * NX + x) * 8 + z, 1),
        ],
        axis=0,
    ).reshape(TOK)
    return (f_grad, own, new_c, new_m)


def solution(mesh):
    in_specs = (
        P(("rep", "cls"), None),
        P("cls", None),
        P("cls", None),
        P("cls"),
        P(("rep", "cls")),
    )
    out_specs = (P(("rep", "cls"), None), P(("rep", "cls")), P("cls", None), P("cls", None))
    return jax.shard_map(local, mesh=mesh, in_specs=in_specs, out_specs=out_specs, check_vma=False)
```

```python
import math

import jax
import jax.numpy as jnp
from jax import lax
from jax.experimental import pallas as pl
from jax.experimental.pallas import tpu as pltpu
from jax.sharding import PartitionSpec as P

MESH = pl.DeviceIdType.MESH

EPS = 1e-06
SCALE = 64.0
MARGIN = 0.35
MOMENT_RATE = 0.9
LEARN_RATE = 0.1

NX, NY, NZ = 2, 4, 8
TOK = 32
HALF = TOK // 2
GROUP = TOK * NX * NY * NZ
D = 512
SLOTS = 1536
ROWS = 2048
SB = 256
NSB = SLOTS // SB
OWN = SLOTS // 2
NCB = OWN // SB
LANES = 128
LOG2E = math.log2(math.e)
F32, BF16 = jnp.float32, jnp.bfloat16


class Sems:
    def __init__(self):
        self.n = 0

    def take(self, count):
        first = self.n
        self.n += count
        return first


_s = Sems()
AG1A, AG1B, AG2B = _s.take(7), _s.take(7), _s.take(7)
AGAP, AGAM = _s.take(8), _s.take(6)
LAB1, LAB2, TA1, TA2, TB1, TB2, POS1, POS2 = (_s.take(7) for _ in range(8))
CORE1, XLO, CORE2 = _s.take(3), _s.take(3), _s.take(3)
RSAP, RSAM, RSB = _s.take(8), _s.take(6), _s.take(3)
RS2A, RSBX, RSBZ = _s.take(7), _s.take(1), _s.take(7)
N_SEMS = _s.n


def wrap(value, n):
    return lax.rem(value + n, n)


def rows16(start, count):
    return pl.ds(pl.multiple_of(start, 16), count)


def lanes(start, count):
    return pl.ds(pl.multiple_of(start, LANES), count)


def fold(values):
    for shift in (64, 32, 16):
        values = values + pltpu.roll(values, shift, 1)
    return values


def row_norm(floats):
    return jnp.sqrt(jnp.sum(floats * floats, axis=-1, keepdims=True) + EPS)


def kernel(
    feat_ref, rowv_ref, lab_ref, rows_ref, cent_hbm, mom_hbm,
    fgrad_ref, loss_ref, crow_hbm, momg_hbm, gsum_hbm,
    cent_v, mom_v, feats, ids_ref, crow, cbf, cbt, momg, expo, soft,
    wide_lab, place, labs, lab1, lab1s, lab2, tot, losses, ta1, ta1s, ta2, tb1, tb1s, tb2, gacc, rtot, pos1, pos1s, pos2,
    csend, cown, crecv, xsend, xrecv, gown,
    ua, ub, sap, rap, sam, ram, sb_, rb_,
    wa, wb, wab, wbb, wbz, wbzb, r2a, rbx, rbz,
    ssem, rsem, lsem,
):
    rep, cls = lax.axis_index("rep"), lax.axis_index("cls")
    x, y, z = lax.div(cls, NY * NZ), lax.rem(lax.div(cls, NZ), NY), lax.rem(cls, NZ)
    x_lo, core = lax.div(rep, 2), lax.rem(rep, 2)

    def at(x, y, z):
        return (rep, (x * NY + y) * NZ + z)

    xy = [(k % NX, k // NX) for k in range(1, NX * NY)]

    def flip(dx):
        return x if dx == 0 else 1 - x

    def xy_to(k):
        dx, dy = xy[k]
        return flip(dx), wrap(y + dy, NY)

    def xy_from(k):
        dx, dy = xy[k]
        return flip(dx), wrap(y - dy, NY)

    def z_to(k):
        return wrap(z + k + 1, NZ)

    def z_from(k):
        return wrap(z - k - 1, NZ)

    xy_peers = [at(*xy_to(k), z) for k in range(7)]
    z_peers = [at(x, y, z_to(k)) for k in range(7)]
    y_peers = [at(x, wrap(y + k + 1, NY), z) for k in range(3)]
    x_peer = at(1 - x, y, z)
    core_peer = (x_lo * 2 + 1 - core, cls)
    xlo_peer = ((1 - x_lo) * 2 + core, cls)
    up_z, down_z = z_peers[0], z_peers[6]

    pending = []

    def push(src, dst, sem, device):
        copy = pltpu.make_async_remote_copy(
            src_ref=src, dst_ref=dst, send_sem=ssem.at[sem], recv_sem=rsem.at[sem],
            device_id=device, device_id_type=MESH,
        )
        copy.start()
        pending.append(copy)

    def arrived(dst, sem):
        pltpu.make_async_remote_copy(
            src_ref=dst, dst_ref=dst, send_sem=ssem.at[sem], recv_sem=rsem.at[sem],
            device_id=core_peer, device_id_type=MESH,
        ).wait_recv()

    stores = []

    def store(src, dst, sem):
        copy = pltpu.make_async_copy(src, dst, lsem.at[sem])
        copy.start()
        stores.append(copy)

    barrier = pltpu.get_barrier_semaphore()
    greet = xy_peers + z_peers + [core_peer, xlo_peer]
    for device in greet:
        pl.semaphore_signal(barrier, inc=1, device_id=device, device_id_type=MESH)

    load_c = pltpu.make_async_copy(cent_hbm, cent_v, lsem.at[0])
    load_m = pltpu.make_async_copy(mom_hbm, mom_v, lsem.at[1])
    load_c.start()
    load_m.start()

    half = GROUP // 2
    my_q, my_b = x * NY + y, y * NX + x

    floats = feat_ref[...].astype(F32)
    unit = (floats / row_norm(floats)).astype(BF16)
    own_a = rows16(z * 128 + my_q * HALF, HALF)
    own_b = rows16(half + my_b * 128 + z * HALF, HALF)
    feats[own_a, :] = unit[:HALF]
    feats[own_b, :] = unit[HALF:]

    lane = lax.broadcasted_iota(jnp.int32, (8, LANES), 1)
    row = lax.broadcasted_iota(jnp.int32, (8, LANES), 0)
    wide_lab[...] = jnp.zeros((8, LANES), jnp.int32)
    wide_lab[0:1, 0:TOK] = lab_ref[...]
    own_lab = jnp.broadcast_to(wide_lab[0:1, :], (8, LANES))
    lab_a = fold(jnp.where(lane < HALF, own_lab, 0))
    lab_b = fold(jnp.where((lane >= HALF) & (lane < TOK), own_lab, 0))
    place[0:8, :] = jnp.where((row == z) & (lax.div(lane, HALF) == my_q), lab_a, 0)
    place[8:16, :] = jnp.where((row == my_b) & (lax.div(lane, HALF) == z), lab_b, 0)

    pl.semaphore_wait(barrier, len(greet))

    for k in range(7):
        push(place, lab1.at[k], LAB1 + k, xy_peers[k])
    for k in range(7):
        push(feats.at[own_a, :], feats.at[own_a, :], AG1A + k, xy_peers[k])
    for k in range(7):
        push(feats.at[own_b, :], feats.at[own_b, :], AG1B + k, z_peers[k])

    for b in range(SLOTS // LANES):
        wide = jnp.broadcast_to(rowv_ref[b : b + 1, :].astype(F32), (LANES, LANES))
        ids_ref[b * LANES : (b + 1) * LANES, :] = wide.T.astype(jnp.int32) + cls * ROWS

    load_c.wait()

    def pick(sb):
        part = slice(sb * SB, (sb + 1) * SB)
        ids = ids_ref[part, :] - cls * ROWS
        col = lax.broadcasted_iota(jnp.int32, (SB, LANES), 1)
        hot = jnp.concatenate(
            [jnp.where(ids == col + j * LANES, 1.0, 0.0).astype(BF16) for j in range(ROWS // LANES)],
            axis=1,
        )
        got = jnp.dot(hot, cent_v[...], preferred_element_type=F32)
        crow[part, :] = got.astype(BF16)
        cbf[part, :] = (got * (1.0 / row_norm(got))).astype(BF16)

    for sb in range(4):
        pick(sb)

    def blk_b(px, py):
        return feats.at[rows16(half + (py * NX + px) * 128, 128), :]

    for k in range(7):
        arrived(lab1.at[k], LAB1 + k)
    lab1s[...] = place[...] + sum(lab1[k] for k in range(7))
    for k in range(7):
        push(lab1s, lab2.at[k], LAB2 + k, z_peers[k])

    for k in range(7):
        px, py = xy_from(k)
        arrived(feats.at[rows16(z * 128 + (px * NY + py) * HALF, HALF), :], AG1A + k)
    def part_of(zb, h):
        return feats.at[rows16(zb * 128 + h * 64, 64), :]

    for h in range(2):
        push(part_of(z, h), part_of(z, h), AGAP + h, up_z)
        push(part_of(z, h), part_of(z, h), AGAM + h, down_z)
    for k in range(7):
        arrived(feats.at[rows16(half + my_b * 128 + z_from(k) * HALF, HALF), :], AG1B + k)
    for k in range(7):
        push(blk_b(x, y), blk_b(x, y), AG2B + k, xy_peers[k])

    for sb in range(4, NSB):
        pick(sb)
    store(crow, crow_hbm, 2)

    def logits(tiles):
        block = jnp.concatenate([feats[rows16(t * LANES, LANES), :] for t in tiles], axis=0)
        rows = [labs[pl.ds(t, 1), :] for t in tiles]
        sums = [jnp.zeros((8, LANES), F32) for _ in range(4)]
        for sb in range(NSB):
            part = slice(sb * SB, (sb + 1) * SB)
            cosine = lax.dot_general(
                cbf[part, :], block, (((1,), (1,)), ((), ())), preferred_element_type=F32
            )
            ids = ids_ref[part, :]
            for h, t in enumerate(tiles):
                cos_h = cosine[:, h * LANES : (h + 1) * LANES]
                match = ids == rows[h]
                logit = SCALE * (cos_h - jnp.where(match, MARGIN, 0.0))
                e = jnp.exp2((logit - SCALE) * LOG2E)
                expo[part, lanes(t * LANES, LANES)] = e
                sums[h] += jnp.sum(e.reshape(SB // 8, 8, LANES), axis=0)
                hit = jnp.where(match, logit, 0.0)
                sums[2 + h] += jnp.sum(hit.reshape(SB // 8, 8, LANES), axis=0)
        for h, t in enumerate(tiles):
            tot[pl.ds(t, 1), :] = jnp.sum(sums[h], axis=0, keepdims=True)
            tot[pl.ds(16 + t, 1), :] = jnp.sum(sums[2 + h], axis=0, keepdims=True)

    def ring(s):
        zp, zm = wrap(z - 1 - s, NZ), wrap(z + 1 + s, NZ)
        for h in range(2):
            p, m = part_of(zp, h), part_of(zm, h)
            arrived(p, AGAP + 2 * s + h)
            if s < 3:
                push(p, p, AGAP + 2 * s + 2 + h, up_z)
                arrived(m, AGAM + 2 * s + h)
            if s < 2:
                push(m, m, AGAM + 2 * s + 2 + h, down_z)
        return zp, zm

    def plane(k):
        px, py = xy_from(k)
        arrived(blk_b(px, py), AG2B + k)
        return 8 + py * NX + px

    load_m.wait()

    def pick_m(j, carry):
        for u in range(16):
            i = j * 16 + u
            momg[pl.ds(i, 1), :] = mom_v[pl.ds(rows_ref[i], 1), :]
        return carry

    def pick_part(part):
        lax.fori_loop(part * SLOTS // 64, (part + 1) * SLOTS // 64, pick_m, 0)

    pick_part(0)
    near = ring(0)
    for k in range(7):
        arrived(lab2.at[k], LAB2 + k)
    labs[...] = lab1s[...] + sum(lab2[k] for k in range(7))
    logits((z, 8 + my_b))
    logits(near)
    pick_part(1)
    pick_part(2)
    near = ring(1)
    logits(near)
    pick_part(3)
    store(momg, momg_hbm, 3)
    for sb in range(NSB):
        cbt[:, sb * SB : (sb + 1) * SB] = cbf[sb * SB : (sb + 1) * SB, :].T
    near = ring(2)
    logits((plane(0), plane(1)))
    logits((plane(2), plane(3)))
    logits((plane(4), plane(5)))
    logits((plane(6), near[1]))

    def push_plane(src, dst, sem):
        for k in range(7):
            push(src, dst.at[k], sem + k, xy_peers[k])

    def push_z(src, dst, sem):
        for k in range(7):
            push(src, dst.at[k], sem + k, z_peers[k])

    def gathered(own, parts, sem):
        for k in range(7):
            arrived(parts.at[k], sem + k)
        return own + sum(parts[k] for k in range(7))

    push_plane(tot.at[8:16, :], tb1, TB1)
    far = ring(3)[0]
    logits((near[0], far))
    push_plane(tot.at[0:8, :], ta1, TA1)
    tb1s[...] = gathered(tot[8:16, :], tb1, TB1)
    push_z(tb1s, tb2, TB2)
    ta1s[...] = gathered(tot[0:8, :], ta1, TA1)
    push_z(ta1s, ta2, TA2)
    push_plane(tot.at[16:32, :], pos1, POS1)

    def soften(first, tiles):
        part = pl.ds(pl.multiple_of(first, SB), SB)
        for t in tiles:
            col = lanes(t * LANES, LANES)
            value = expo[part, col] * rtot[pl.ds(t, 1), :]
            match = jnp.where(ids_ref[part, :] == labs[pl.ds(t, 1), :], 1.0, 0.0)
            soft[part, col] = (value - match).astype(BF16)

    def feature_part(tiles):
        cols = jnp.concatenate([soft[:, lanes(t * LANES, LANES)] for t in tiles], axis=1)
        return SCALE * jnp.dot(cbt[...], cols, preferred_element_type=F32)

    def center_half_b(first):
        part = pl.ds(pl.multiple_of(first, SB), SB)
        gacc[part, :] = jnp.dot(soft[part, half:], feats[half:, :], preferred_element_type=F32)

    def center_grad(first):
        soften(first, range(8))
        part = pl.ds(pl.multiple_of(first, SB), SB)
        grad = jnp.dot(soft[part, :half], feats[:half, :], preferred_element_type=F32)
        return (SCALE * (gacc[part, :] + grad)).astype(BF16)

    mine, other = core * OWN, (1 - core) * OWN

    def grad_other(i):
        csend[i] = center_grad(other + i * SB)
        push(csend.at[i], crecv.at[i], CORE1 + i, core_peer)

    def grad_mine(i):
        cown[i] = center_grad(mine + i * SB)

    def join_cores(i):
        arrived(crecv.at[i], CORE1 + i)
        xsend[i] = (cown[i].astype(F32) + crecv[i].astype(F32)).astype(BF16)
        push(xsend.at[i], xrecv.at[i], XLO + i, xlo_peer)

    def tiles_a(s):
        return wrap(z + 4 - s, NZ), wrap(z - 3 + s, NZ)

    def tiles_b(yb):
        return 8 + yb * NX, 8 + yb * NX + 1

    def ring_sum(s):
        for h in range(2):
            part = slice(h * 256, (h + 1) * 256)
            plus = ua[s, part, :128]
            if s:
                arrived(rap.at[s - 1, part], RSAP + 2 * s - 2 + h)
                plus = plus + rap[s - 1, part].astype(F32)
            sap[s, part] = plus.astype(BF16)
            push(sap.at[s, part], rap.at[s, part], RSAP + 2 * s + h, up_z)
            if s < 3:
                minus = ua[s, part, 128:]
                if s:
                    arrived(ram.at[s - 1, part], RSAM + 2 * s - 2 + h)
                    minus = minus + ram[s - 1, part].astype(F32)
                sam[s, part] = minus.astype(BF16)
                push(sam.at[s, part], ram.at[s, part], RSAM + 2 * s + h, down_z)

    def part_a(s):
        ua[s] = feature_part(tiles_a(s))

    y_to = [wrap(y + k + 1, NY) for k in range(3)]

    def send_b(k):
        sb_[k] = feature_part(tiles_b(y_to[k])).astype(BF16)
        push(sb_.at[k], rb_.at[k], RSB + k, y_peers[k])

    totals_b = gathered(tb1s[...], tb2, TB2)
    rtot[8:16, :] = 1.0 / totals_b
    for k in (1, 0, 2):
        for sb in range(NSB):
            soften(sb * SB, tiles_b(y_to[k]))
        send_b(k)
    for sb in range(NSB):
        soften(sb * SB, tiles_b(y))
    for sb in range(NSB):
        center_half_b(sb * SB)

    totals_a = gathered(ta1s[...], ta2, TA2)
    rtot[0:8, :] = 1.0 / totals_a
    grad_other(0)
    grad_mine(0)
    for i in range(1, NCB):
        soften(other + i * SB, tiles_a(0))
        soften(mine + i * SB, tiles_a(0))
    part_a(0)
    ring_sum(0)
    grad_other(1)
    grad_mine(1)
    join_cores(0)
    grad_other(2)
    grad_mine(2)
    part_a(1)
    pos1s[...] = gathered(tot[16:32, :], pos1, POS1)
    push_z(pos1s, pos2, POS2)
    join_cores(1)
    ring_sum(1)
    join_cores(2)
    part_a(2)
    part_a(3)
    ub[...] = feature_part(tiles_b(y))
    ring_sum(2)

    positive = gathered(pos1s[...], pos2, POS2)
    losses[0:8, :] = jnp.log(totals_a) + SCALE - positive[:8]
    losses[8:16, :] = jnp.log(totals_b) + SCALE - positive[8:]
    lane = lax.broadcasted_iota(jnp.int32, (8, LANES), 1)
    loss_a = jnp.broadcast_to(losses[pl.ds(z, 1), :], (8, LANES))
    loss_b = jnp.broadcast_to(losses[pl.ds(8 + my_b, 1), :], (8, LANES))
    loss_a = fold(jnp.where(lax.div(lane, HALF) == my_q, loss_a, 0.0))
    loss_b = fold(jnp.where(lax.div(lane, HALF) == z, loss_b, 0.0))
    loss_ref[...] = jnp.where(lane < HALF, loss_a, loss_b)

    def finish_center(i):
        arrived(xrecv.at[i], XLO + i)
        gown[i] = (xsend[i].astype(F32) + xrecv[i].astype(F32)).astype(BF16)
        place_i = gsum_hbm.at[rows16(mine + i * SB, SB), :]
        push(gown.at[i], place_i, CORE2 + i, core_peer)
        store(gown.at[i], place_i, 4 + i)

    finish_center(0)
    ring_sum(3)

    for k in range(3):
        arrived(rb_.at[k], RSB + k)
    slab = ub[...] + sum(rb_[k].astype(F32) for k in range(3))
    for h in range(2):
        turned = slab[:, h * 128 : (h + 1) * 128].T
        for q in range(NZ):
            wb[q * TOK + h * HALF : q * TOK + (h + 1) * HALF, :] = turned[q * HALF : (q + 1) * HALF, :]
    wbb[...] = wb[...].astype(BF16)
    for k in range(7):
        push(wbb.at[rows16(z_to(k) * TOK, TOK), :], rbz.at[k], RSBZ + k, z_peers[k])

    finish_center(1)

    for h in range(2):
        part = slice(h * 256, (h + 1) * 256)
        arrived(ram.at[2, part], RSAM + 4 + h)
        arrived(rap.at[3, part], RSAP + 6 + h)
    slab = ua[3][:, 128:] + rap[3].astype(F32) + ram[2].astype(F32)
    wa[...] = slab.T
    wab[...] = wa[...].astype(BF16)
    for k in range(7):
        px, py = xy_to(k)
        push(wab.at[rows16((px * NY + py) * HALF, HALF), :], r2a.at[k], RS2A + k, xy_peers[k])

    for k in range(7):
        arrived(rbz.at[k], RSBZ + k)
    wbz[...] = wb[rows16(z * TOK, TOK), :] + sum(rbz[k].astype(F32) for k in range(7))
    wbzb[...] = wbz[rows16((1 - x) * HALF, HALF), :].astype(BF16)
    push(wbzb, rbx, RSBX, x_peer)

    finish_center(2)

    for k in range(7):
        arrived(r2a.at[k], RS2A + k)
    g_a = wa[rows16(my_q * HALF, HALF), :] + sum(r2a[k].astype(F32) for k in range(7))
    arrived(rbx, RSBX)
    g_b = wbz[rows16(x * HALF, HALF), :] + rbx[...].astype(F32)
    for h, grad in enumerate((g_a, g_b)):
        own = feat_ref[h * HALF : (h + 1) * HALF, :].astype(F32)
        norm = row_norm(own)
        unit_f = own / norm
        dot = jnp.sum(unit_f * grad, axis=1, keepdims=True)
        fgrad_ref[h * HALF : (h + 1) * HALF, :] = (grad - unit_f * dot) / norm

    for i in range(NCB):
        arrived(gsum_hbm.at[rows16(other + i * SB, SB), :], CORE2 + i)
    for copy in pending:
        copy.wait_send()
    for copy in stores:
        copy.wait()


def update(
    crow_hbm, momg_hbm, gsum_hbm, fgrad_hbm, loss_ref, newc_hbm, newm_hbm, fout_hbm, lout_ref,
    rows_v, mom_v, grad_v, newc_v, newm_v, sem,
):
    n = SLOTS // SB
    pass_on = pltpu.make_async_copy(fgrad_hbm, fout_hbm, sem.at[5 * n])
    pass_on.start()

    def part(i):
        return pl.ds(i * SB, SB)

    loads, stores = [], []
    for i in range(n):
        for j, (src, dst) in enumerate(((crow_hbm, rows_v), (gsum_hbm, grad_v), (momg_hbm, mom_v))):
            copy = pltpu.make_async_copy(src.at[part(i), :], dst.at[part(i), :], sem.at[j * n + i])
            copy.start()
            loads.append(copy)
    lout_ref[...] = loss_ref[0:1, 0:TOK]
    for i in range(n):
        for copy in loads[3 * i : 3 * i + 3]:
            copy.wait()
        rows, grad = rows_v[part(i), :].astype(F32), grad_v[part(i), :].astype(F32)
        inverse = 1.0 / row_norm(rows)
        along = jnp.sum(rows * grad, axis=1, keepdims=True) * (inverse * inverse * inverse)
        new_m = MOMENT_RATE * mom_v[part(i), :] + (grad * inverse - rows * along)
        newm_v[part(i), :] = new_m
        newc_v[part(i), :] = (rows - LEARN_RATE * new_m).astype(BF16)
        for j, (src, dst) in enumerate(((newm_v, newm_hbm), (newc_v, newc_hbm))):
            copy = pltpu.make_async_copy(src.at[part(i), :], dst.at[part(i), :], sem.at[(3 + j) * n + i])
            copy.start()
            stores.append(copy)
    for copy in stores:
        copy.wait()
    pass_on.wait()


def local(features, centers, momentum, sample_rows, labels):
    vm = pl.BlockSpec(memory_space=pltpu.VMEM)
    hbm = pl.BlockSpec(memory_space=pl.ANY)
    v = pltpu.VMEM
    sds = jax.ShapeDtypeStruct
    f_grad, loss, crow, momg, gsum = pl.pallas_call(
        kernel,
        out_shape=(
            sds((TOK, D), F32),
            sds((8, LANES), F32),
            sds((SLOTS, D), BF16),
            sds((SLOTS, D), F32),
            sds((SLOTS, D), BF16),
        ),
        in_specs=[vm, vm, vm, pl.BlockSpec(memory_space=pltpu.SMEM), hbm, hbm],
        out_specs=(vm, vm, hbm, hbm, hbm),
        scratch_shapes=[
            v((ROWS, D), BF16), v((ROWS, D), F32), v((GROUP, D), BF16), v((SLOTS, LANES), jnp.int32),
            v((SLOTS, D), BF16), v((SLOTS, D), BF16), v((D, SLOTS), BF16), v((SLOTS, D), F32),
            v((SLOTS, GROUP), F32), v((SLOTS, GROUP), BF16),
            v((8, LANES), jnp.int32), v((16, LANES), jnp.int32), v((16, LANES), jnp.int32),
            v((7, 16, LANES), jnp.int32),
            v((16, LANES), jnp.int32), v((7, 16, LANES), jnp.int32),
            v((32, LANES), F32), v((16, LANES), F32),
            v((7, 8, LANES), F32), v((8, LANES), F32), v((7, 8, LANES), F32),
            v((7, 8, LANES), F32), v((8, LANES), F32), v((7, 8, LANES), F32), v((SLOTS, D), F32),
            v((16, LANES), F32), v((7, 16, LANES), F32), v((16, LANES), F32), v((7, 16, LANES), F32),
            v((NCB, SB, D), BF16), v((NCB, SB, D), BF16), v((NCB, SB, D), BF16),
            v((NCB, SB, D), BF16), v((NCB, SB, D), BF16), v((NCB, SB, D), BF16),
            v((4, D, 256), F32), v((D, 256), F32),
            v((4, D, 128), BF16), v((4, D, 128), BF16), v((3, D, 128), BF16), v((3, D, 128), BF16),
            v((3, D, 256), BF16), v((3, D, 256), BF16),
            v((128, D), F32), v((256, D), F32), v((128, D), BF16), v((256, D), BF16),
            v((TOK, D), F32), v((HALF, D), BF16),
            v((7, HALF, D), BF16), v((HALF, D), BF16), v((7, TOK, D), BF16),
            pltpu.SemaphoreType.DMA((N_SEMS,)), pltpu.SemaphoreType.DMA((N_SEMS,)),
            pltpu.SemaphoreType.DMA((4 + NCB,)),
        ],
        compiler_params=pltpu.CompilerParams(
            collective_id=0, has_side_effects=True, vmem_limit_bytes=60 * 1024 * 1024
        ),
    )(
        features,
        sample_rows.reshape(SLOTS // LANES, LANES),
        labels.reshape(1, TOK),
        sample_rows,
        centers,
        momentum,
    )
    new_c, new_m, f_grad, loss = pl.pallas_call(
        update,
        out_shape=(
            sds((SLOTS, D), BF16), sds((SLOTS, D), F32), sds((TOK, D), F32), sds((1, TOK), F32),
        ),
        in_specs=[hbm, hbm, hbm, hbm, vm],
        out_specs=(hbm, hbm, hbm, vm),
        scratch_shapes=[
            v((SLOTS, D), BF16), v((SLOTS, D), F32), v((SLOTS, D), BF16),
            v((SLOTS, D), BF16), v((SLOTS, D), F32),
            pltpu.SemaphoreType.DMA((5 * NSB + 1,)),
        ],
        compiler_params=pltpu.CompilerParams(vmem_limit_bytes=60 * 1024 * 1024),
    )(crow, momg, gsum, f_grad, loss)
    return (f_grad, loss.reshape(TOK), new_c, new_m)


def solution(mesh):
    in_specs = (
        P(("rep", "cls"), None),
        P("cls", None),
        P("cls", None),
        P("cls"),
        P(("rep", "cls")),
    )
    out_specs = (P(("rep", "cls"), None), P(("rep", "cls")), P("cls", None), P("cls", None))
    return jax.shard_map(local, mesh=mesh, in_specs=in_specs, out_specs=out_specs, check_vma=False)
```

```python
import math

import jax
import jax.numpy as jnp
from jax import lax
from jax.experimental import pallas as pl
from jax.experimental.pallas import tpu as pltpu
from jax.sharding import PartitionSpec as P

MESH = pl.DeviceIdType.MESH

EPS = 1e-06
SCALE = 64.0
MARGIN = 0.35
MOMENT_RATE = 0.9
LEARN_RATE = 0.1

NX, NY, NZ = 2, 4, 8
TOK = 32
HALF = TOK // 2
GROUP = TOK * NX * NY * NZ
D = 512
SLOTS = 1536
ROWS = 2048
SB = 256
NSB = SLOTS // SB
OWN = SLOTS // 2
NCB = OWN // SB
UB = 512
LANES = 128
LOG2E = math.log2(math.e)
F32, BF16 = jnp.float32, jnp.bfloat16


class Sems:
    def __init__(self):
        self.n = 0

    def take(self, count):
        first = self.n
        self.n += count
        return first


_s = Sems()
AG1A, AG1B, AG2B = _s.take(7), _s.take(7), _s.take(7)
AGAP, AGAM = _s.take(8), _s.take(6)
LAB1, LAB2, TOT1, TOT2, POS1, POS2 = (_s.take(7) for _ in range(6))
CORE1, XLO, CORE2 = _s.take(3), _s.take(3), _s.take(3)
RSAP, RSAM, RSB = _s.take(8), _s.take(6), _s.take(3)
RS2A, RSBX, RSBZ = _s.take(7), _s.take(1), _s.take(7)
N_SEMS = _s.n


def wrap(value, n):
    return lax.rem(value + n, n)


def rows16(start, count):
    return pl.ds(pl.multiple_of(start, 16), count)


def lanes(start, count):
    return pl.ds(pl.multiple_of(start, LANES), count)


def fold(values):
    for shift in (64, 32, 16):
        values = values + pltpu.roll(values, shift, 1)
    return values


def row_norm(floats):
    return jnp.sqrt(jnp.sum(floats * floats, axis=-1, keepdims=True) + EPS)


def kernel(
    feat_ref, rowv_ref, lab_ref, rows_ref, cent_hbm, mom_hbm,
    fgrad_ref, loss_ref, crow_hbm, momg_hbm, gsum_hbm,
    cent_v, mom_v, feats, ids_ref, crow, cbf, cbt, momg, expo, soft,
    wide_lab, place, labs, lab1, lab1s, lab2, tot, losses, tot1, tot1s, tot2, rtot, pm1, pos1, pos1s, pos2,
    csend, cown, crecv, xsend, xrecv, gown,
    up, mm, sap, rap, sam, ram, sb_, rb_,
    wa, wb, wab, wbb, wbz, wbzb, r2a, rbx, rbz,
    ssem, rsem, lsem,
):
    rep, cls = lax.axis_index("rep"), lax.axis_index("cls")
    x, y, z = lax.div(cls, NY * NZ), lax.rem(lax.div(cls, NZ), NY), lax.rem(cls, NZ)
    x_lo, core = lax.div(rep, 2), lax.rem(rep, 2)

    def at(x, y, z):
        return (rep, (x * NY + y) * NZ + z)

    xy = [(k % NX, k // NX) for k in range(1, NX * NY)]

    def flip(dx):
        return x if dx == 0 else 1 - x

    def xy_to(k):
        dx, dy = xy[k]
        return flip(dx), wrap(y + dy, NY)

    def xy_from(k):
        dx, dy = xy[k]
        return flip(dx), wrap(y - dy, NY)

    def z_to(k):
        return wrap(z + k + 1, NZ)

    def z_from(k):
        return wrap(z - k - 1, NZ)

    xy_peers = [at(*xy_to(k), z) for k in range(7)]
    z_peers = [at(x, y, z_to(k)) for k in range(7)]
    y_peers = [at(x, wrap(y + k + 1, NY), z) for k in range(3)]
    x_peer = at(1 - x, y, z)
    core_peer = (x_lo * 2 + 1 - core, cls)
    xlo_peer = ((1 - x_lo) * 2 + core, cls)
    up_z, down_z = z_peers[0], z_peers[6]

    pending = []

    def push(src, dst, sem, device):
        copy = pltpu.make_async_remote_copy(
            src_ref=src, dst_ref=dst, send_sem=ssem.at[sem], recv_sem=rsem.at[sem],
            device_id=device, device_id_type=MESH,
        )
        copy.start()
        pending.append(copy)

    def arrived(dst, sem):
        pltpu.make_async_remote_copy(
            src_ref=dst, dst_ref=dst, send_sem=ssem.at[sem], recv_sem=rsem.at[sem],
            device_id=core_peer, device_id_type=MESH,
        ).wait_recv()

    stores = []

    def store(src, dst, sem):
        copy = pltpu.make_async_copy(src, dst, lsem.at[sem])
        copy.start()
        stores.append(copy)

    barrier = pltpu.get_barrier_semaphore()
    greet = xy_peers + z_peers + [core_peer, xlo_peer]
    for device in greet:
        pl.semaphore_signal(barrier, inc=1, device_id=device, device_id_type=MESH)

    load_c = pltpu.make_async_copy(cent_hbm, cent_v, lsem.at[0])
    load_m = pltpu.make_async_copy(mom_hbm, mom_v, lsem.at[1])
    load_c.start()
    load_m.start()

    half = GROUP // 2
    my_q, my_b = x * NY + y, y * NX + x

    floats = feat_ref[...].astype(F32)
    unit = (floats / row_norm(floats)).astype(BF16)
    own_a = rows16(z * 128 + my_q * HALF, HALF)
    own_b = rows16(half + my_b * 128 + z * HALF, HALF)
    feats[own_a, :] = unit[:HALF]
    feats[own_b, :] = unit[HALF:]

    lane = lax.broadcasted_iota(jnp.int32, (8, LANES), 1)
    row = lax.broadcasted_iota(jnp.int32, (8, LANES), 0)
    wide_lab[...] = jnp.zeros((8, LANES), jnp.int32)
    wide_lab[0:1, 0:TOK] = lab_ref[...]
    own_lab = jnp.broadcast_to(wide_lab[0:1, :], (8, LANES))
    lab_a = fold(jnp.where(lane < HALF, own_lab, 0))
    lab_b = fold(jnp.where((lane >= HALF) & (lane < TOK), own_lab, 0))
    place[0:8, :] = jnp.where((row == z) & (lax.div(lane, HALF) == my_q), lab_a, 0)
    place[8:16, :] = jnp.where((row == my_b) & (lax.div(lane, HALF) == z), lab_b, 0)

    pl.semaphore_wait(barrier, len(greet))

    for k in range(7):
        push(place, lab1.at[k], LAB1 + k, xy_peers[k])
    for k in range(7):
        push(feats.at[own_a, :], feats.at[own_a, :], AG1A + k, xy_peers[k])
    for k in range(7):
        push(feats.at[own_b, :], feats.at[own_b, :], AG1B + k, z_peers[k])

    for b in range(SLOTS // LANES):
        wide = jnp.broadcast_to(rowv_ref[b : b + 1, :].astype(F32), (LANES, LANES))
        ids_ref[b * LANES : (b + 1) * LANES, :] = wide.T.astype(jnp.int32) + cls * ROWS

    load_c.wait()

    def pick(sb):
        part = slice(sb * SB, (sb + 1) * SB)
        ids = ids_ref[part, :] - cls * ROWS
        col = lax.broadcasted_iota(jnp.int32, (SB, LANES), 1)
        hot = jnp.concatenate(
            [jnp.where(ids == col + j * LANES, 1.0, 0.0).astype(BF16) for j in range(ROWS // LANES)],
            axis=1,
        )
        got = jnp.dot(hot, cent_v[...], preferred_element_type=F32)
        crow[part, :] = got.astype(BF16)
        cbf[part, :] = (got * (1.0 / row_norm(got))).astype(BF16)

    for sb in range(4):
        pick(sb)

    def blk_b(px, py):
        return feats.at[rows16(half + (py * NX + px) * 128, 128), :]

    for k in range(7):
        arrived(lab1.at[k], LAB1 + k)
    lab1s[...] = place[...] + sum(lab1[k] for k in range(7))
    for k in range(7):
        push(lab1s, lab2.at[k], LAB2 + k, z_peers[k])

    for k in range(7):
        px, py = xy_from(k)
        arrived(feats.at[rows16(z * 128 + (px * NY + py) * HALF, HALF), :], AG1A + k)
    def part_of(zb, h):
        return feats.at[rows16(zb * 128 + h * 64, 64), :]

    for h in range(2):
        push(part_of(z, h), part_of(z, h), AGAP + h, up_z)
        push(part_of(z, h), part_of(z, h), AGAM + h, down_z)
    for k in range(7):
        arrived(feats.at[rows16(half + my_b * 128 + z_from(k) * HALF, HALF), :], AG1B + k)
    for k in range(7):
        push(blk_b(x, y), blk_b(x, y), AG2B + k, xy_peers[k])

    for sb in range(4, NSB):
        pick(sb)
    store(crow, crow_hbm, 2)

    def logits(tiles):
        block = jnp.concatenate([feats[rows16(t * LANES, LANES), :] for t in tiles], axis=0)
        rows = [labs[pl.ds(t, 1), :] for t in tiles]
        sums = [jnp.zeros((8, LANES), F32) for _ in range(4)]
        for sb in range(NSB):
            part = slice(sb * SB, (sb + 1) * SB)
            cosine = lax.dot_general(
                cbf[part, :], block, (((1,), (1,)), ((), ())), preferred_element_type=F32
            )
            ids = ids_ref[part, :]
            for h, t in enumerate(tiles):
                cos_h = cosine[:, h * LANES : (h + 1) * LANES]
                match = ids == rows[h]
                logit = SCALE * (cos_h - jnp.where(match, MARGIN, 0.0))
                e = jnp.exp2((logit - SCALE) * LOG2E)
                expo[part, lanes(t * LANES, LANES)] = e
                soft[part, lanes(t * LANES, LANES)] = jnp.where(match, 0.0, e).astype(BF16)
                sums[h] += jnp.sum(e.reshape(SB // 8, 8, LANES), axis=0)
                hit = jnp.where(match, logit, 0.0)
                sums[2 + h] += jnp.sum(hit.reshape(SB // 8, 8, LANES), axis=0)
        for h, t in enumerate(tiles):
            tot[pl.ds(t, 1), :] = jnp.sum(sums[h], axis=0, keepdims=True)
            tot[pl.ds(16 + t, 1), :] = jnp.sum(sums[2 + h], axis=0, keepdims=True)

    def ring(s):
        zp, zm = wrap(z - 1 - s, NZ), wrap(z + 1 + s, NZ)
        for h in range(2):
            p, m = part_of(zp, h), part_of(zm, h)
            arrived(p, AGAP + 2 * s + h)
            if s < 3:
                push(p, p, AGAP + 2 * s + 2 + h, up_z)
                arrived(m, AGAM + 2 * s + h)
            if s < 2:
                push(m, m, AGAM + 2 * s + 2 + h, down_z)
        return zp, zm

    def plane(k):
        px, py = xy_from(k)
        arrived(blk_b(px, py), AG2B + k)
        return 8 + py * NX + px

    load_m.wait()

    def pick_m(j, carry):
        for u in range(16):
            i = j * 16 + u
            momg[pl.ds(i, 1), :] = mom_v[pl.ds(rows_ref[i], 1), :]
        return carry

    def pick_part(part):
        lax.fori_loop(part * SLOTS // 64, (part + 1) * SLOTS // 64, pick_m, 0)

    pick_part(0)
    near = ring(0)
    for k in range(7):
        arrived(lab2.at[k], LAB2 + k)
    labs[...] = lab1s[...] + sum(lab2[k] for k in range(7))
    logits((z, 8 + my_b))
    logits(near)
    pick_part(1)
    pick_part(2)
    near = ring(1)
    logits(near)
    pick_part(3)
    store(momg, momg_hbm, 3)
    for sb in range(NSB):
        cbt[:, sb * SB : (sb + 1) * SB] = cbf[sb * SB : (sb + 1) * SB, :].T
    near = ring(2)
    logits((plane(0), plane(1)))
    logits((plane(2), plane(3)))
    logits((plane(4), plane(5)))
    logits((plane(6), near[1]))

    def push_plane(src, dst, sem):
        for k in range(7):
            push(src, dst.at[k], sem + k, xy_peers[k])

    def push_z(src, dst, sem):
        for k in range(7):
            push(src, dst.at[k], sem + k, z_peers[k])

    def gathered(own, parts, sem):
        for k in range(7):
            arrived(parts.at[k], sem + k)
        return own + sum(parts[k] for k in range(7))

    far = ring(3)[0]
    logits((near[0], far))
    push_plane(tot.at[0:16, :], tot1, TOT1)

    def other_classes(k):
        col = slice(k * 256, (k + 1) * 256)
        up[:, col] = jnp.dot(cbt[...], soft[:, col], preferred_element_type=F32)

    def label_center(k):
        col = slice(k * 256, (k + 1) * 256)
        rows = [labs[2 * k + h : 2 * k + h + 1, :] for h in range(2)]
        match = jnp.concatenate(
            [jnp.where(ids_ref[...] == r, 1.0, 0.0).astype(BF16) for r in rows], axis=1
        )
        mm[:, col] = jnp.dot(cbt[...], match, preferred_element_type=F32).astype(BF16)

    for k in range(8):
        other_classes(k)
    tot1s[...] = gathered(tot[0:16, :], tot1, TOT1)
    push_z(tot1s, tot2, TOT2)
    push_plane(tot.at[16:32, :], pos1, POS1)
    for k in range(8):
        label_center(k)
    totals = gathered(tot1s[...], tot2, TOT2)
    rtot[...] = 1.0 / totals
    pm1[...] = jnp.exp2((tot[16:32, :] - SCALE) * LOG2E) * rtot[...] - 1.0

    def soften(first, tiles):
        part = pl.ds(pl.multiple_of(first, SB), SB)
        for t in tiles:
            col = lanes(t * LANES, LANES)
            value = expo[part, col] * rtot[pl.ds(t, 1), :]
            match = jnp.where(ids_ref[part, :] == labs[pl.ds(t, 1), :], 1.0, 0.0)
            soft[part, col] = (value - match).astype(BF16)

    def feature_part(t):
        col, row = lanes(t * LANES, LANES), pl.ds(t, 1)
        return SCALE * (up[:, col] * rtot[row, :] + mm[:, col].astype(F32) * pm1[row, :])

    def center_grad(first):
        soften(first, range(GROUP // LANES))
        part = pl.ds(pl.multiple_of(first, SB), SB)
        return (SCALE * jnp.dot(soft[part, :], feats[...], preferred_element_type=F32)).astype(BF16)

    mine, other = core * OWN, (1 - core) * OWN

    def grad_other(i):
        csend[i] = center_grad(other + i * SB)
        push(csend.at[i], crecv.at[i], CORE1 + i, core_peer)

    def grad_mine(i):
        cown[i] = center_grad(mine + i * SB)

    def join_cores(i):
        arrived(crecv.at[i], CORE1 + i)
        xsend[i] = (cown[i].astype(F32) + crecv[i].astype(F32)).astype(BF16)
        push(xsend.at[i], xrecv.at[i], XLO + i, xlo_peer)

    def tiles_a(s):
        return wrap(z + 4 - s, NZ), wrap(z - 3 + s, NZ)

    def tiles_b(yb):
        return 8 + yb * NX, 8 + yb * NX + 1

    def ring_sum(s):
        tp, tm = tiles_a(s)
        plus_all, minus_all = feature_part(tp), feature_part(tm) if s < 3 else None
        for h in range(2):
            part = slice(h * 256, (h + 1) * 256)
            plus = plus_all[part]
            if s:
                arrived(rap.at[s - 1, part], RSAP + 2 * s - 2 + h)
                plus = plus + rap[s - 1, part].astype(F32)
            sap[s, part] = plus.astype(BF16)
            push(sap.at[s, part], rap.at[s, part], RSAP + 2 * s + h, up_z)
            if s < 3:
                minus = minus_all[part]
                if s:
                    arrived(ram.at[s - 1, part], RSAM + 2 * s - 2 + h)
                    minus = minus + ram[s - 1, part].astype(F32)
                sam[s, part] = minus.astype(BF16)
                push(sam.at[s, part], ram.at[s, part], RSAM + 2 * s + h, down_z)

    y_to = [wrap(y + k + 1, NY) for k in range(3)]

    def send_b(k):
        for h, t in enumerate(tiles_b(y_to[k])):
            sb_[k, :, h * LANES : (h + 1) * LANES] = feature_part(t).astype(BF16)
        push(sb_.at[k], rb_.at[k], RSB + k, y_peers[k])

    ring_sum(0)
    send_b(1)
    send_b(0)
    send_b(2)
    grad_other(0)
    grad_mine(0)
    grad_other(1)
    join_cores(0)
    ring_sum(1)
    grad_mine(1)
    grad_other(2)
    join_cores(1)
    pos1s[...] = gathered(tot[16:32, :], pos1, POS1)
    push_z(pos1s, pos2, POS2)
    grad_mine(2)
    ring_sum(2)
    join_cores(2)

    positive = gathered(pos1s[...], pos2, POS2)
    losses[...] = jnp.log(totals) + SCALE - positive
    lane = lax.broadcasted_iota(jnp.int32, (8, LANES), 1)
    loss_a = jnp.broadcast_to(losses[pl.ds(z, 1), :], (8, LANES))
    loss_b = jnp.broadcast_to(losses[pl.ds(8 + my_b, 1), :], (8, LANES))
    loss_a = fold(jnp.where(lax.div(lane, HALF) == my_q, loss_a, 0.0))
    loss_b = fold(jnp.where(lax.div(lane, HALF) == z, loss_b, 0.0))
    loss_ref[...] = jnp.where(lane < HALF, loss_a, loss_b)

    def finish_center(i):
        arrived(xrecv.at[i], XLO + i)
        gown[i] = (xsend[i].astype(F32) + xrecv[i].astype(F32)).astype(BF16)
        place_i = gsum_hbm.at[rows16(mine + i * SB, SB), :]
        push(gown.at[i], place_i, CORE2 + i, core_peer)
        store(gown.at[i], place_i, 4 + i)

    finish_center(0)
    ring_sum(3)

    for k in range(3):
        arrived(rb_.at[k], RSB + k)
    for h, t in enumerate(tiles_b(y)):
        slab = feature_part(t) + sum(rb_[k, :, h * LANES : (h + 1) * LANES].astype(F32) for k in range(3))
        turned = slab.T
        for q in range(NZ):
            wb[q * TOK + h * HALF : q * TOK + (h + 1) * HALF, :] = turned[q * HALF : (q + 1) * HALF, :]
    wbb[...] = wb[...].astype(BF16)
    for k in range(7):
        push(wbb.at[rows16(z_to(k) * TOK, TOK), :], rbz.at[k], RSBZ + k, z_peers[k])

    finish_center(1)

    for h in range(2):
        part = slice(h * 256, (h + 1) * 256)
        arrived(ram.at[2, part], RSAM + 4 + h)
        arrived(rap.at[3, part], RSAP + 6 + h)
    slab = feature_part(z) + rap[3].astype(F32) + ram[2].astype(F32)
    wa[...] = slab.T
    wab[...] = wa[...].astype(BF16)
    for k in range(7):
        px, py = xy_to(k)
        push(wab.at[rows16((px * NY + py) * HALF, HALF), :], r2a.at[k], RS2A + k, xy_peers[k])

    for k in range(7):
        arrived(rbz.at[k], RSBZ + k)
    wbz[...] = wb[rows16(z * TOK, TOK), :] + sum(rbz[k].astype(F32) for k in range(7))
    wbzb[...] = wbz[rows16((1 - x) * HALF, HALF), :].astype(BF16)
    push(wbzb, rbx, RSBX, x_peer)

    finish_center(2)

    for k in range(7):
        arrived(r2a.at[k], RS2A + k)
    g_a = wa[rows16(my_q * HALF, HALF), :] + sum(r2a[k].astype(F32) for k in range(7))
    arrived(rbx, RSBX)
    g_b = wbz[rows16(x * HALF, HALF), :] + rbx[...].astype(F32)
    for h, grad in enumerate((g_a, g_b)):
        own = feat_ref[h * HALF : (h + 1) * HALF, :].astype(F32)
        norm = row_norm(own)
        unit_f = own / norm
        dot = jnp.sum(unit_f * grad, axis=1, keepdims=True)
        fgrad_ref[h * HALF : (h + 1) * HALF, :] = (grad - unit_f * dot) / norm

    for i in range(NCB):
        arrived(gsum_hbm.at[rows16(other + i * SB, SB), :], CORE2 + i)
    for copy in pending:
        copy.wait_send()
    for copy in stores:
        copy.wait()


def update(
    crow_hbm, momg_hbm, gsum_hbm, fgrad_hbm, loss_ref, newc_hbm, newm_hbm, fout_hbm, lout_ref,
    rows_v, mom_v, grad_v, newc_v, newm_v, sem,
):
    n = SLOTS // UB
    pass_on = pltpu.make_async_copy(fgrad_hbm, fout_hbm, sem.at[5 * n])
    pass_on.start()

    def part(i):
        return pl.ds(i * UB, UB)

    loads, stores = [], []
    for i in range(n):
        for j, (src, dst) in enumerate(((crow_hbm, rows_v), (gsum_hbm, grad_v), (momg_hbm, mom_v))):
            copy = pltpu.make_async_copy(src.at[part(i), :], dst.at[part(i), :], sem.at[j * n + i])
            copy.start()
            loads.append(copy)
    lout_ref[...] = loss_ref[0:1, 0:TOK]
    for i in range(n):
        for copy in loads[3 * i : 3 * i + 3]:
            copy.wait()
        rows, grad = rows_v[part(i), :].astype(F32), grad_v[part(i), :].astype(F32)
        inverse = 1.0 / row_norm(rows)
        along = jnp.sum(rows * grad, axis=1, keepdims=True) * (inverse * inverse * inverse)
        new_m = MOMENT_RATE * mom_v[part(i), :] + (grad * inverse - rows * along)
        newm_v[part(i), :] = new_m
        newc_v[part(i), :] = (rows - LEARN_RATE * new_m).astype(BF16)
        for j, (src, dst) in enumerate(((newm_v, newm_hbm), (newc_v, newc_hbm))):
            copy = pltpu.make_async_copy(src.at[part(i), :], dst.at[part(i), :], sem.at[(3 + j) * n + i])
            copy.start()
            stores.append(copy)
    for copy in stores:
        copy.wait()
    pass_on.wait()


def local(features, centers, momentum, sample_rows, labels):
    vm = pl.BlockSpec(memory_space=pltpu.VMEM)
    hbm = pl.BlockSpec(memory_space=pl.ANY)
    v = pltpu.VMEM
    sds = jax.ShapeDtypeStruct
    f_grad, loss, crow, momg, gsum = pl.pallas_call(
        kernel,
        out_shape=(
            sds((TOK, D), F32),
            sds((8, LANES), F32),
            sds((SLOTS, D), BF16),
            sds((SLOTS, D), F32),
            sds((SLOTS, D), BF16),
        ),
        in_specs=[vm, vm, vm, pl.BlockSpec(memory_space=pltpu.SMEM), hbm, hbm],
        out_specs=(vm, vm, hbm, hbm, hbm),
        scratch_shapes=[
            v((ROWS, D), BF16), v((ROWS, D), F32), v((GROUP, D), BF16), v((SLOTS, LANES), jnp.int32),
            v((SLOTS, D), BF16), v((SLOTS, D), BF16), v((D, SLOTS), BF16), v((SLOTS, D), F32),
            v((SLOTS, GROUP), F32), v((SLOTS, GROUP), BF16),
            v((8, LANES), jnp.int32), v((16, LANES), jnp.int32), v((16, LANES), jnp.int32),
            v((7, 16, LANES), jnp.int32),
            v((16, LANES), jnp.int32), v((7, 16, LANES), jnp.int32),
            v((32, LANES), F32), v((16, LANES), F32),
            v((7, 16, LANES), F32), v((16, LANES), F32), v((7, 16, LANES), F32), v((16, LANES), F32),
            v((16, LANES), F32), v((7, 16, LANES), F32), v((16, LANES), F32), v((7, 16, LANES), F32),
            v((NCB, SB, D), BF16), v((NCB, SB, D), BF16), v((NCB, SB, D), BF16),
            v((NCB, SB, D), BF16), v((NCB, SB, D), BF16), v((NCB, SB, D), BF16),
            v((D, GROUP), F32), v((D, GROUP), BF16),
            v((4, D, 128), BF16), v((4, D, 128), BF16), v((3, D, 128), BF16), v((3, D, 128), BF16),
            v((3, D, 256), BF16), v((3, D, 256), BF16),
            v((128, D), F32), v((256, D), F32), v((128, D), BF16), v((256, D), BF16),
            v((TOK, D), F32), v((HALF, D), BF16),
            v((7, HALF, D), BF16), v((HALF, D), BF16), v((7, TOK, D), BF16),
            pltpu.SemaphoreType.DMA((N_SEMS,)), pltpu.SemaphoreType.DMA((N_SEMS,)),
            pltpu.SemaphoreType.DMA((4 + NCB,)),
        ],
        compiler_params=pltpu.CompilerParams(
            collective_id=0, has_side_effects=True, vmem_limit_bytes=60 * 1024 * 1024
        ),
    )(
        features,
        sample_rows.reshape(SLOTS // LANES, LANES),
        labels.reshape(1, TOK),
        sample_rows,
        centers,
        momentum,
    )
    new_c, new_m, f_grad, loss = pl.pallas_call(
        update,
        out_shape=(
            sds((SLOTS, D), BF16), sds((SLOTS, D), F32), sds((TOK, D), F32), sds((1, TOK), F32),
        ),
        in_specs=[hbm, hbm, hbm, hbm, vm],
        out_specs=(hbm, hbm, hbm, vm),
        scratch_shapes=[
            v((SLOTS, D), BF16), v((SLOTS, D), F32), v((SLOTS, D), BF16),
            v((SLOTS, D), BF16), v((SLOTS, D), F32),
            pltpu.SemaphoreType.DMA((5 * (SLOTS // UB) + 1,)),
        ],
        compiler_params=pltpu.CompilerParams(vmem_limit_bytes=60 * 1024 * 1024),
    )(crow, momg, gsum, f_grad, loss)
    return (f_grad, loss.reshape(TOK), new_c, new_m)


def solution(mesh):
    in_specs = (
        P(("rep", "cls"), None),
        P("cls", None),
        P("cls", None),
        P("cls"),
        P(("rep", "cls")),
    )
    out_specs = (P(("rep", "cls"), None), P(("rep", "cls")), P("cls", None), P("cls", None))
    return jax.shard_map(local, mesh=mesh, in_specs=in_specs, out_specs=out_specs, check_vma=False)
```

```python
import math

import jax
import jax.numpy as jnp
from jax import lax
from jax.experimental import pallas as pl
from jax.experimental.pallas import tpu as pltpu
from jax.sharding import PartitionSpec as P

MESH = pl.DeviceIdType.MESH

EPS = 1e-06
SCALE = 64.0
MARGIN = 0.35
MOMENT_RATE = 0.9
LEARN_RATE = 0.1

NX, NY, NZ = 2, 4, 8
TOK = 32
HALF = TOK // 2
GROUP = TOK * NX * NY * NZ
D = 512
SLOTS = 1536
ROWS = 2048
SB = 256
NSB = SLOTS // SB
OWN = SLOTS // 2
NCB = OWN // SB
UB = 512
LANES = 128
LOG2E = math.log2(math.e)
F32, BF16 = jnp.float32, jnp.bfloat16


class Sems:
    def __init__(self):
        self.n = 0

    def take(self, count):
        first = self.n
        self.n += count
        return first


_s = Sems()
AG1A, AG1B, AG2B = _s.take(7), _s.take(7), _s.take(7)
AGAP, AGAM = _s.take(8), _s.take(6)
LAB1, LAB2, TOT1, TOT2, POS1, POS2 = (_s.take(7) for _ in range(6))
CORE1, XLO, CORE2 = _s.take(3), _s.take(3), _s.take(3)
RSAP, RSAM, RSB = _s.take(8), _s.take(6), _s.take(3)
RS2A, RSBX, RSBZ = _s.take(7), _s.take(1), _s.take(7)
N_SEMS = _s.n


def wrap(value, n):
    return lax.rem(value + n, n)


def rows16(start, count):
    return pl.ds(pl.multiple_of(start, 16), count)


def lanes(start, count):
    return pl.ds(pl.multiple_of(start, LANES), count)


def fold(values):
    for shift in (64, 32, 16):
        values = values + pltpu.roll(values, shift, 1)
    return values


def row_norm(floats):
    return jnp.sqrt(jnp.sum(floats * floats, axis=-1, keepdims=True) + EPS)


def kernel(
    feat_ref, rowv_ref, lab_ref, rows_ref, cent_hbm, mom_hbm,
    fgrad_ref, loss_ref, crow_hbm, momg_hbm, gsum_hbm,
    cent_v, mom_v, feats, ids_ref, crow, cbf, cbt, momg, expo, soft,
    wide_lab, place, labs, lab1, lab1s, lab2, tot, losses, tot1, tot1s, tot2, rtot, pm1, pos1, pos1s, pos2,
    csend, cown, crecv, xsend, xrecv, gown,
    up, mm, sap, rap, sam, ram, sb_, rb_,
    wa, wb, wab, wbb, wbz, wbzb, r2a, rbx, rbz,
    ssem, rsem, lsem,
):
    rep, cls = lax.axis_index("rep"), lax.axis_index("cls")
    x, y, z = lax.div(cls, NY * NZ), lax.rem(lax.div(cls, NZ), NY), lax.rem(cls, NZ)
    x_lo, core = lax.div(rep, 2), lax.rem(rep, 2)

    def at(x, y, z):
        return (rep, (x * NY + y) * NZ + z)

    xy = [(k % NX, k // NX) for k in range(1, NX * NY)]

    def flip(dx):
        return x if dx == 0 else 1 - x

    def xy_to(k):
        dx, dy = xy[k]
        return flip(dx), wrap(y + dy, NY)

    def xy_from(k):
        dx, dy = xy[k]
        return flip(dx), wrap(y - dy, NY)

    def z_to(k):
        return wrap(z + k + 1, NZ)

    def z_from(k):
        return wrap(z - k - 1, NZ)

    xy_peers = [at(*xy_to(k), z) for k in range(7)]
    z_peers = [at(x, y, z_to(k)) for k in range(7)]
    y_peers = [at(x, wrap(y + k + 1, NY), z) for k in range(3)]
    x_peer = at(1 - x, y, z)
    core_peer = (x_lo * 2 + 1 - core, cls)
    xlo_peer = ((1 - x_lo) * 2 + core, cls)
    up_z, down_z = z_peers[0], z_peers[6]

    pending = []

    def push(src, dst, sem, device):
        copy = pltpu.make_async_remote_copy(
            src_ref=src, dst_ref=dst, send_sem=ssem.at[sem], recv_sem=rsem.at[sem],
            device_id=device, device_id_type=MESH,
        )
        copy.start()
        pending.append(copy)

    def arrived(dst, sem):
        pltpu.make_async_remote_copy(
            src_ref=dst, dst_ref=dst, send_sem=ssem.at[sem], recv_sem=rsem.at[sem],
            device_id=core_peer, device_id_type=MESH,
        ).wait_recv()

    stores = []

    def store(src, dst, sem):
        copy = pltpu.make_async_copy(src, dst, lsem.at[sem])
        copy.start()
        stores.append(copy)

    barrier = pltpu.get_barrier_semaphore()
    greet = xy_peers + z_peers + [core_peer, xlo_peer]
    for device in greet:
        pl.semaphore_signal(barrier, inc=1, device_id=device, device_id_type=MESH)

    load_c = pltpu.make_async_copy(cent_hbm, cent_v, lsem.at[0])
    load_m = pltpu.make_async_copy(mom_hbm, mom_v, lsem.at[1])
    load_c.start()
    load_m.start()

    half = GROUP // 2
    my_q, my_b = x * NY + y, y * NX + x

    floats = feat_ref[...].astype(F32)
    unit = (floats / row_norm(floats)).astype(BF16)
    own_a = rows16(z * 128 + my_q * HALF, HALF)
    own_b = rows16(half + my_b * 128 + z * HALF, HALF)
    feats[own_a, :] = unit[:HALF]
    feats[own_b, :] = unit[HALF:]

    lane = lax.broadcasted_iota(jnp.int32, (8, LANES), 1)
    row = lax.broadcasted_iota(jnp.int32, (8, LANES), 0)
    wide_lab[...] = jnp.zeros((8, LANES), jnp.int32)
    wide_lab[0:1, 0:TOK] = lab_ref[...]
    own_lab = jnp.broadcast_to(wide_lab[0:1, :], (8, LANES))
    lab_a = fold(jnp.where(lane < HALF, own_lab, 0))
    lab_b = fold(jnp.where((lane >= HALF) & (lane < TOK), own_lab, 0))
    place[0:8, :] = jnp.where((row == z) & (lax.div(lane, HALF) == my_q), lab_a, 0)
    place[8:16, :] = jnp.where((row == my_b) & (lax.div(lane, HALF) == z), lab_b, 0)

    pl.semaphore_wait(barrier, len(greet))

    for k in range(7):
        push(place, lab1.at[k], LAB1 + k, xy_peers[k])
    for k in range(7):
        push(feats.at[own_a, :], feats.at[own_a, :], AG1A + k, xy_peers[k])
    for k in range(7):
        push(feats.at[own_b, :], feats.at[own_b, :], AG1B + k, z_peers[k])

    for b in range(SLOTS // LANES):
        wide = jnp.broadcast_to(rowv_ref[b : b + 1, :].astype(F32), (LANES, LANES))
        ids_ref[b * LANES : (b + 1) * LANES, :] = wide.T.astype(jnp.int32) + cls * ROWS

    load_c.wait()

    def pick(sb):
        part = slice(sb * SB, (sb + 1) * SB)
        ids = ids_ref[part, :] - cls * ROWS
        col = lax.broadcasted_iota(jnp.int32, (SB, LANES), 1)
        hot = jnp.concatenate(
            [jnp.where(ids == col + j * LANES, 1.0, 0.0).astype(BF16) for j in range(ROWS // LANES)],
            axis=1,
        )
        got = jnp.dot(hot, cent_v[...], preferred_element_type=F32)
        crow[part, :] = got.astype(BF16)
        cbf[part, :] = (got * (1.0 / row_norm(got))).astype(BF16)

    for sb in range(4):
        pick(sb)

    def blk_b(px, py):
        return feats.at[rows16(half + (py * NX + px) * 128, 128), :]

    for k in range(7):
        arrived(lab1.at[k], LAB1 + k)
    lab1s[...] = place[...] + sum(lab1[k] for k in range(7))
    for k in range(7):
        push(lab1s, lab2.at[k], LAB2 + k, z_peers[k])

    for k in range(7):
        px, py = xy_from(k)
        arrived(feats.at[rows16(z * 128 + (px * NY + py) * HALF, HALF), :], AG1A + k)
    def part_of(zb, h):
        return feats.at[rows16(zb * 128 + h * 64, 64), :]

    for h in range(2):
        push(part_of(z, h), part_of(z, h), AGAP + h, up_z)
        push(part_of(z, h), part_of(z, h), AGAM + h, down_z)
    for k in range(7):
        arrived(feats.at[rows16(half + my_b * 128 + z_from(k) * HALF, HALF), :], AG1B + k)
    for k in range(7):
        push(blk_b(x, y), blk_b(x, y), AG2B + k, xy_peers[k])

    for sb in range(4, NSB):
        pick(sb)
    store(crow, crow_hbm, 2)
    for sb in range(NSB):
        cbt[:, sb * SB : (sb + 1) * SB] = cbf[sb * SB : (sb + 1) * SB, :].T

    def logits(tiles):
        block = jnp.concatenate([feats[rows16(t * LANES, LANES), :] for t in tiles], axis=0)
        rows = [labs[pl.ds(t, 1), :] for t in tiles]
        sums = [jnp.zeros((8, LANES), F32) for _ in range(4)]
        for sb in range(NSB):
            part = slice(sb * SB, (sb + 1) * SB)
            cosine = lax.dot_general(
                cbf[part, :], block, (((1,), (1,)), ((), ())), preferred_element_type=F32
            )
            ids = ids_ref[part, :]
            for h, t in enumerate(tiles):
                cos_h = cosine[:, h * LANES : (h + 1) * LANES]
                match = ids == rows[h]
                logit = SCALE * (cos_h - jnp.where(match, MARGIN, 0.0))
                e = jnp.exp2((logit - SCALE) * LOG2E)
                expo[part, lanes(t * LANES, LANES)] = e
                soft[part, lanes(t * LANES, LANES)] = jnp.where(match, 0.0, e).astype(BF16)
                sums[h] += jnp.sum(e.reshape(SB // 8, 8, LANES), axis=0)
                hit = jnp.where(match, logit, 0.0)
                sums[2 + h] += jnp.sum(hit.reshape(SB // 8, 8, LANES), axis=0)
        for h, t in enumerate(tiles):
            tot[pl.ds(t, 1), :] = jnp.sum(sums[h], axis=0, keepdims=True)
            tot[pl.ds(16 + t, 1), :] = jnp.sum(sums[2 + h], axis=0, keepdims=True)

    def ring(s):
        zp, zm = wrap(z - 1 - s, NZ), wrap(z + 1 + s, NZ)
        for h in range(2):
            p, m = part_of(zp, h), part_of(zm, h)
            arrived(p, AGAP + 2 * s + h)
            if s < 3:
                push(p, p, AGAP + 2 * s + 2 + h, up_z)
                arrived(m, AGAM + 2 * s + h)
            if s < 2:
                push(m, m, AGAM + 2 * s + 2 + h, down_z)
        return zp, zm

    def plane(k):
        px, py = xy_from(k)
        arrived(blk_b(px, py), AG2B + k)
        return 8 + py * NX + px

    def label_center(k):
        col = slice(k * 256, (k + 1) * 256)
        rows = [labs[2 * k + h : 2 * k + h + 1, :] for h in range(2)]
        match = jnp.concatenate(
            [jnp.where(ids_ref[...] == r, 1.0, 0.0).astype(BF16) for r in rows], axis=1
        )
        mm[:, col] = jnp.dot(cbt[...], match, preferred_element_type=F32).astype(BF16)

    near = ring(0)
    for k in range(7):
        arrived(lab2.at[k], LAB2 + k)
    labs[...] = lab1s[...] + sum(lab2[k] for k in range(7))
    logits((z, 8 + my_b))
    logits(near)
    label_center(0)
    label_center(1)
    near = ring(1)
    logits(near)
    label_center(2)
    label_center(3)
    label_center(4)
    near = ring(2)
    logits((plane(0), plane(1)))
    logits((plane(2), plane(3)))
    logits((plane(4), plane(5)))
    logits((plane(6), near[1]))

    def push_plane(src, dst, sem):
        for k in range(7):
            push(src, dst.at[k], sem + k, xy_peers[k])

    def push_z(src, dst, sem):
        for k in range(7):
            push(src, dst.at[k], sem + k, z_peers[k])

    def gathered(own, parts, sem):
        for k in range(7):
            arrived(parts.at[k], sem + k)
        return own + sum(parts[k] for k in range(7))

    far = ring(3)[0]
    logits((near[0], far))
    push_plane(tot.at[0:16, :], tot1, TOT1)

    def other_classes(k):
        col = slice(k * 256, (k + 1) * 256)
        up[:, col] = jnp.dot(cbt[...], soft[:, col], preferred_element_type=F32)

    for k in range(8):
        other_classes(k)
    tot1s[...] = gathered(tot[0:16, :], tot1, TOT1)
    push_z(tot1s, tot2, TOT2)
    push_plane(tot.at[16:32, :], pos1, POS1)
    for k in range(5, 8):
        label_center(k)
    totals = gathered(tot1s[...], tot2, TOT2)
    rtot[...] = 1.0 / totals
    pm1[...] = jnp.exp2((tot[16:32, :] - SCALE) * LOG2E) * rtot[...] - 1.0

    def soften(first, tiles):
        part = pl.ds(pl.multiple_of(first, SB), SB)
        for t in tiles:
            col = lanes(t * LANES, LANES)
            value = expo[part, col] * rtot[pl.ds(t, 1), :]
            match = jnp.where(ids_ref[part, :] == labs[pl.ds(t, 1), :], 1.0, 0.0)
            soft[part, col] = (value - match).astype(BF16)

    def feature_part(t):
        col, row = lanes(t * LANES, LANES), pl.ds(t, 1)
        return SCALE * (up[:, col] * rtot[row, :] + mm[:, col].astype(F32) * pm1[row, :])

    def center_grad(first):
        soften(first, range(GROUP // LANES))
        part = pl.ds(pl.multiple_of(first, SB), SB)
        return (SCALE * jnp.dot(soft[part, :], feats[...], preferred_element_type=F32)).astype(BF16)

    mine, other = core * OWN, (1 - core) * OWN

    def grad_other(i):
        csend[i] = center_grad(other + i * SB)
        push(csend.at[i], crecv.at[i], CORE1 + i, core_peer)

    def grad_mine(i):
        cown[i] = center_grad(mine + i * SB)

    def join_cores(i):
        arrived(crecv.at[i], CORE1 + i)
        xsend[i] = (cown[i].astype(F32) + crecv[i].astype(F32)).astype(BF16)
        push(xsend.at[i], xrecv.at[i], XLO + i, xlo_peer)

    def tiles_a(s):
        return wrap(z + 4 - s, NZ), wrap(z - 3 + s, NZ)

    def tiles_b(yb):
        return 8 + yb * NX, 8 + yb * NX + 1

    def ring_sum(s):
        tp, tm = tiles_a(s)
        plus_all, minus_all = feature_part(tp), feature_part(tm) if s < 3 else None
        for h in range(2):
            part = slice(h * 256, (h + 1) * 256)
            plus = plus_all[part]
            if s:
                arrived(rap.at[s - 1, part], RSAP + 2 * s - 2 + h)
                plus = plus + rap[s - 1, part].astype(F32)
            sap[s, part] = plus.astype(BF16)
            push(sap.at[s, part], rap.at[s, part], RSAP + 2 * s + h, up_z)
            if s < 3:
                minus = minus_all[part]
                if s:
                    arrived(ram.at[s - 1, part], RSAM + 2 * s - 2 + h)
                    minus = minus + ram[s - 1, part].astype(F32)
                sam[s, part] = minus.astype(BF16)
                push(sam.at[s, part], ram.at[s, part], RSAM + 2 * s + h, down_z)

    y_to = [wrap(y + k + 1, NY) for k in range(3)]

    def send_b(k):
        for h, t in enumerate(tiles_b(y_to[k])):
            sb_[k, :, h * LANES : (h + 1) * LANES] = feature_part(t).astype(BF16)
        push(sb_.at[k], rb_.at[k], RSB + k, y_peers[k])

    load_m.wait()

    def pick_m(j, carry):
        for u in range(16):
            i = j * 16 + u
            momg[pl.ds(i, 1), :] = mom_v[pl.ds(rows_ref[i], 1), :]
        return carry

    def pick_part(part):
        lax.fori_loop(part * SLOTS // 64, (part + 1) * SLOTS // 64, pick_m, 0)

    ring_sum(0)
    send_b(1)
    send_b(0)
    send_b(2)
    grad_other(0)
    grad_mine(0)
    grad_other(1)
    join_cores(0)
    ring_sum(1)
    grad_mine(1)
    grad_other(2)
    join_cores(1)
    pos1s[...] = gathered(tot[16:32, :], pos1, POS1)
    push_z(pos1s, pos2, POS2)
    grad_mine(2)
    ring_sum(2)
    join_cores(2)
    pick_part(0)
    pick_part(1)

    positive = gathered(pos1s[...], pos2, POS2)
    losses[...] = jnp.log(totals) + SCALE - positive
    lane = lax.broadcasted_iota(jnp.int32, (8, LANES), 1)
    loss_a = jnp.broadcast_to(losses[pl.ds(z, 1), :], (8, LANES))
    loss_b = jnp.broadcast_to(losses[pl.ds(8 + my_b, 1), :], (8, LANES))
    loss_a = fold(jnp.where(lax.div(lane, HALF) == my_q, loss_a, 0.0))
    loss_b = fold(jnp.where(lax.div(lane, HALF) == z, loss_b, 0.0))
    loss_ref[...] = jnp.where(lane < HALF, loss_a, loss_b)

    def finish_center(i):
        arrived(xrecv.at[i], XLO + i)
        gown[i] = (xsend[i].astype(F32) + xrecv[i].astype(F32)).astype(BF16)
        place_i = gsum_hbm.at[rows16(mine + i * SB, SB), :]
        push(gown.at[i], place_i, CORE2 + i, core_peer)
        store(gown.at[i], place_i, 4 + i)

    finish_center(0)
    ring_sum(3)
    pick_part(2)

    for k in range(3):
        arrived(rb_.at[k], RSB + k)
    for h, t in enumerate(tiles_b(y)):
        slab = feature_part(t) + sum(rb_[k, :, h * LANES : (h + 1) * LANES].astype(F32) for k in range(3))
        turned = slab.T
        for q in range(NZ):
            wb[q * TOK + h * HALF : q * TOK + (h + 1) * HALF, :] = turned[q * HALF : (q + 1) * HALF, :]
    wbb[...] = wb[...].astype(BF16)
    for k in range(7):
        push(wbb.at[rows16(z_to(k) * TOK, TOK), :], rbz.at[k], RSBZ + k, z_peers[k])

    pick_part(3)
    store(momg, momg_hbm, 3)
    finish_center(1)

    for h in range(2):
        part = slice(h * 256, (h + 1) * 256)
        arrived(ram.at[2, part], RSAM + 4 + h)
        arrived(rap.at[3, part], RSAP + 6 + h)
    slab = feature_part(z) + rap[3].astype(F32) + ram[2].astype(F32)
    wa[...] = slab.T
    wab[...] = wa[...].astype(BF16)
    for k in range(7):
        px, py = xy_to(k)
        push(wab.at[rows16((px * NY + py) * HALF, HALF), :], r2a.at[k], RS2A + k, xy_peers[k])

    for k in range(7):
        arrived(rbz.at[k], RSBZ + k)
    wbz[...] = wb[rows16(z * TOK, TOK), :] + sum(rbz[k].astype(F32) for k in range(7))
    wbzb[...] = wbz[rows16((1 - x) * HALF, HALF), :].astype(BF16)
    push(wbzb, rbx, RSBX, x_peer)

    finish_center(2)

    for k in range(7):
        arrived(r2a.at[k], RS2A + k)
    g_a = wa[rows16(my_q * HALF, HALF), :] + sum(r2a[k].astype(F32) for k in range(7))
    arrived(rbx, RSBX)
    g_b = wbz[rows16(x * HALF, HALF), :] + rbx[...].astype(F32)
    for h, grad in enumerate((g_a, g_b)):
        own = feat_ref[h * HALF : (h + 1) * HALF, :].astype(F32)
        norm = row_norm(own)
        unit_f = own / norm
        dot = jnp.sum(unit_f * grad, axis=1, keepdims=True)
        fgrad_ref[h * HALF : (h + 1) * HALF, :] = (grad - unit_f * dot) / norm

    for i in range(NCB):
        arrived(gsum_hbm.at[rows16(other + i * SB, SB), :], CORE2 + i)
    for copy in pending:
        copy.wait_send()
    for copy in stores:
        copy.wait()


def update(
    crow_hbm, momg_hbm, gsum_hbm, fgrad_hbm, loss_ref, newc_hbm, newm_hbm, fout_hbm, lout_ref,
    rows_v, mom_v, grad_v, newc_v, newm_v, sem,
):
    n = SLOTS // UB
    pass_on = pltpu.make_async_copy(fgrad_hbm, fout_hbm, sem.at[5 * n])
    pass_on.start()

    def part(i):
        return pl.ds(i * UB, UB)

    loads, stores = [], []
    for i in range(n):
        for j, (src, dst) in enumerate(((crow_hbm, rows_v), (gsum_hbm, grad_v), (momg_hbm, mom_v))):
            copy = pltpu.make_async_copy(src.at[part(i), :], dst.at[part(i), :], sem.at[j * n + i])
            copy.start()
            loads.append(copy)
    lout_ref[...] = loss_ref[0:1, 0:TOK]
    for i in range(n):
        for copy in loads[3 * i : 3 * i + 3]:
            copy.wait()
        rows, grad = rows_v[part(i), :].astype(F32), grad_v[part(i), :].astype(F32)
        inverse = 1.0 / row_norm(rows)
        along = jnp.sum(rows * grad, axis=1, keepdims=True) * (inverse * inverse * inverse)
        new_m = MOMENT_RATE * mom_v[part(i), :] + (grad * inverse - rows * along)
        newm_v[part(i), :] = new_m
        newc_v[part(i), :] = (rows - LEARN_RATE * new_m).astype(BF16)
        for j, (src, dst) in enumerate(((newm_v, newm_hbm), (newc_v, newc_hbm))):
            copy = pltpu.make_async_copy(src.at[part(i), :], dst.at[part(i), :], sem.at[(3 + j) * n + i])
            copy.start()
            stores.append(copy)
    for copy in stores:
        copy.wait()
    pass_on.wait()


def local(features, centers, momentum, sample_rows, labels):
    vm = pl.BlockSpec(memory_space=pltpu.VMEM)
    hbm = pl.BlockSpec(memory_space=pl.ANY)
    v = pltpu.VMEM
    sds = jax.ShapeDtypeStruct
    f_grad, loss, crow, momg, gsum = pl.pallas_call(
        kernel,
        out_shape=(
            sds((TOK, D), F32),
            sds((8, LANES), F32),
            sds((SLOTS, D), BF16),
            sds((SLOTS, D), F32),
            sds((SLOTS, D), BF16),
        ),
        in_specs=[vm, vm, vm, pl.BlockSpec(memory_space=pltpu.SMEM), hbm, hbm],
        out_specs=(vm, vm, hbm, hbm, hbm),
        scratch_shapes=[
            v((ROWS, D), BF16), v((ROWS, D), F32), v((GROUP, D), BF16), v((SLOTS, LANES), jnp.int32),
            v((SLOTS, D), BF16), v((SLOTS, D), BF16), v((D, SLOTS), BF16), v((SLOTS, D), F32),
            v((SLOTS, GROUP), F32), v((SLOTS, GROUP), BF16),
            v((8, LANES), jnp.int32), v((16, LANES), jnp.int32), v((16, LANES), jnp.int32),
            v((7, 16, LANES), jnp.int32),
            v((16, LANES), jnp.int32), v((7, 16, LANES), jnp.int32),
            v((32, LANES), F32), v((16, LANES), F32),
            v((7, 16, LANES), F32), v((16, LANES), F32), v((7, 16, LANES), F32), v((16, LANES), F32),
            v((16, LANES), F32), v((7, 16, LANES), F32), v((16, LANES), F32), v((7, 16, LANES), F32),
            v((NCB, SB, D), BF16), v((NCB, SB, D), BF16), v((NCB, SB, D), BF16),
            v((NCB, SB, D), BF16), v((NCB, SB, D), BF16), v((NCB, SB, D), BF16),
            v((D, GROUP), F32), v((D, GROUP), BF16),
            v((4, D, 128), BF16), v((4, D, 128), BF16), v((3, D, 128), BF16), v((3, D, 128), BF16),
            v((3, D, 256), BF16), v((3, D, 256), BF16),
            v((128, D), F32), v((256, D), F32), v((128, D), BF16), v((256, D), BF16),
            v((TOK, D), F32), v((HALF, D), BF16),
            v((7, HALF, D), BF16), v((HALF, D), BF16), v((7, TOK, D), BF16),
            pltpu.SemaphoreType.DMA((N_SEMS,)), pltpu.SemaphoreType.DMA((N_SEMS,)),
            pltpu.SemaphoreType.DMA((4 + NCB,)),
        ],
        compiler_params=pltpu.CompilerParams(
            collective_id=0, has_side_effects=True, vmem_limit_bytes=60 * 1024 * 1024
        ),
    )(
        features,
        sample_rows.reshape(SLOTS // LANES, LANES),
        labels.reshape(1, TOK),
        sample_rows,
        centers,
        momentum,
    )
    new_c, new_m, f_grad, loss = pl.pallas_call(
        update,
        out_shape=(
            sds((SLOTS, D), BF16), sds((SLOTS, D), F32), sds((TOK, D), F32), sds((1, TOK), F32),
        ),
        in_specs=[hbm, hbm, hbm, hbm, vm],
        out_specs=(hbm, hbm, hbm, vm),
        scratch_shapes=[
            v((SLOTS, D), BF16), v((SLOTS, D), F32), v((SLOTS, D), BF16),
            v((SLOTS, D), BF16), v((SLOTS, D), F32),
            pltpu.SemaphoreType.DMA((5 * (SLOTS // UB) + 1,)),
        ],
        compiler_params=pltpu.CompilerParams(vmem_limit_bytes=60 * 1024 * 1024),
    )(crow, momg, gsum, f_grad, loss)
    return (f_grad, loss.reshape(TOK), new_c, new_m)


def solution(mesh):
    in_specs = (
        P(("rep", "cls"), None),
        P("cls", None),
        P("cls", None),
        P("cls"),
        P(("rep", "cls")),
    )
    out_specs = (P(("rep", "cls"), None), P(("rep", "cls")), P("cls", None), P("cls", None))
    return jax.shard_map(local, mesh=mesh, in_specs=in_specs, out_specs=out_specs, check_vma=False)
```
